32 devices in a mesh: row: 8 (over y, x, core), col: 4 (over z).
Axes of the slice: x: 2, y: 2, z: 4, core: 2. Of those that a mesh axis runs over, the one named last changes fastest.
Arguments:
- hidden_in: bfloat16 [2048, 7168], P('row'), may hold values from -6 to 6
- norm_gain: float32 [7168], replicated, may hold values from 0.5 to 1.5
- norm_bias: float32 [7168], replicated, may hold values from -3 to 3
- w_query: bfloat16 [7168, 6144], P('row', 'col'), may hold values from -0.0625 to 0.0625
- w_keyval: bfloat16 [7168, 2, 6144], P('row', None, 'col'), may hold values from -0.125 to 0.125
- bias_query: float32 [6144], P('col'), may hold values from -3 to 3
- bias_keyval: float32 [2, 6144], P(None, 'col'), may hold values from -3 to 3
- cache_keys: bfloat16 [8, 4096, 6144], P('row', None, 'col'), may hold values from -60 to 60
- cache_values: bfloat16 [8, 4096, 6144], P('row', None, 'col'), may hold values from -12 to 12
- cache_lengths: int32 [8], replicated, may hold values from 2 to 4096
- owner_slot: int32 [8], replicated, may hold values from 0 to 7, each once
- w_out: bfloat16 [6144, 7168], P('col', 'row'), may hold values from -0.3125 to 0.3125
- bias_out: float32 [7168], P('col'), may hold values from -3 to 3
Outputs:
- hidden_out: bfloat16 [2048, 7168], P('row', 'col')
- new_keys: bfloat16 [8, 256, 6144], P('row', None, 'col')
- new_values: bfloat16 [8, 256, 6144], P('row', None, 'col')
The draws below stay inside these ranges and needn't reach their ends.
Inputs may be any that keep to these rules, and one draw needn't show every extreme that they name: `owner_slot`: each slot is the owner of exactly one request.
All inputs are finite; a program needn't handle non-finite values.
Results may differ from the reference program's by a relative error of at most 0.01375.
Values may be sent and summed in bfloat16 or wider, within the bound.
No kernel may reach another device: no remote copies, remote signals or barrier semaphores. Data moves between devices by JAX's collectives and lax.ppermute only.
A program may use at most 192 MiB of HBM per device.

```python
import jax
import jax.numpy as jnp
from jax import lax

D = 7168
HEADS = 48
HEAD = 128
GROUP = 256
CACHE = 4096
HD = 6144
REQS = 8
TOKENS = 2048


def draw_cache_lengths(key, part):
    key_one, key_two, key_three, key_four = jax.random.split(jax.random.fold_in(key, 11), 4)
    first_draw = jax.random.randint(key_one, (REQS,), 2, CACHE + 1)
    second_draw = jax.random.randint(key_two, (REQS,), 2, CACHE + 1)
    lengths = jnp.minimum(first_draw, second_draw)
    longest = jax.random.randint(key_three, (), 0, REQS)
    shortest = (longest + jax.random.randint(key_four, (), 1, REQS)) % REQS
    slot_ids = jnp.arange(REQS)
    lengths = jnp.where(slot_ids == longest, CACHE, jnp.where(slot_ids == shortest, 2, lengths))
    return lengths.astype(jnp.int32)


def draw_cache_keys(key, part):
    key_one = jax.random.fold_in(jax.random.fold_in(key, 23), 0)
    result = jnp.clip(2.0 * jax.random.normal(key_one, (REQS, CACHE, HD), jnp.float32), -12.0, 12.0)
    return result.astype(jnp.bfloat16)


def steps_of(own_key, dims, pieces, least, top_value):
    def one(axis_at, shards_of):
        heights = jax.random.uniform(jax.random.fold_in(jax.random.fold_in(own_key, 6), axis_at), (shards_of,), jnp.float32, least / len(pieces), top_value / len(pieces))
        return jnp.repeat(jnp.exp(heights), dims[axis_at] // shards_of).reshape((-1,) + (1,) * (len(dims) - axis_at - 1))

    factor_of = one(*pieces[0])
    for cut in pieces[1:]:
        factor_of = factor_of * one(*cut)
    return factor_of


def noise(key, shape, deviation, bound, cuts=(), held_as=jnp.bfloat16):
    values = deviation * jax.random.normal(key, shape, jnp.float32)
    if cuts:
        values = values * steps_of(key, shape, cuts, -0.22, 0.18)
    return jnp.clip(values, -bound, bound).astype(held_as)


def setup_inputs(seed: int = 0) -> dict:
    arg_keys = jax.random.split(jax.random.key(seed), 14)
    return {
        "hidden_in": noise(arg_keys[0], (TOKENS, D), 1.0, 6.0, ((0, 8),)),
        "norm_gain": jnp.clip(1.0 + 0.1 * jax.random.normal(arg_keys[1], (D,), jnp.float32), 0.5, 1.5),
        "norm_bias": noise(arg_keys[2], (D,), 0.5, 3.0, (), jnp.float32),
        "w_query": noise(arg_keys[3], (D, HD), D ** -0.5, 0.0625, ((0, 8), (1, 4))),
        "w_keyval": noise(arg_keys[4], (D, 2, HD), (D // 4) ** -0.5, 0.125, ((0, 8), (2, 4))),
        "bias_query": noise(arg_keys[5], (HD,), 0.5, 3.0, ((0, 4),), jnp.float32),
        "bias_keyval": noise(arg_keys[6], (2, HD), 0.5, 3.0, ((1, 4),), jnp.float32),
        "cache_keys": draw_cache_keys(jax.random.fold_in(arg_keys[13], 71), 0),
        "cache_values": noise(arg_keys[8], (REQS, CACHE, HD), 2.0, 12.0, ((0, 8), (2, 4))),
        "cache_lengths": draw_cache_lengths(jax.random.fold_in(arg_keys[13], 71), 0),
        "owner_slot": jax.random.permutation(arg_keys[10], REQS).astype(jnp.int32),
        "w_out": noise(arg_keys[11], (HD, D), (HD // 16) ** -0.5, 0.3125, ((0, 4), (1, 8))),
        "bias_out": noise(arg_keys[12], (D,), 0.5, 3.0, ((0, 4),), jnp.float32),
    }


def normalize(inputs, gain, bias):
    row_mean = lax.optimization_barrier(jnp.mean(inputs, axis=-1, keepdims=True))
    centered = inputs - row_mean
    row_var = lax.optimization_barrier(jnp.mean(centered * centered, axis=-1, keepdims=True))
    return centered * lax.rsqrt(row_var + 1e-05) * gain + bias

def reference(hidden_in, norm_gain, norm_bias, w_query, w_keyval, bias_query, bias_keyval, cache_keys, cache_values, cache_lengths, owner_slot, w_out, bias_out):
    inputs = hidden_in.astype(jnp.float32)
    normed = normalize(inputs, norm_gain, norm_bias).astype(jnp.bfloat16)
    q_scale = HEAD ** (-0.5)
    query_all = ((jnp.dot(normed, w_query, preferred_element_type=jnp.float32) + bias_query) * q_scale).astype(jnp.bfloat16)
    keyval = (jnp.dot(normed, w_keyval.reshape(D, 2 * HD), preferred_element_type=jnp.float32) + bias_keyval.reshape(2 * HD)).astype(jnp.bfloat16)
    keys_all = keyval[:, :HD]
    values_all = keyval[:, HD:]
    slot_ids = jnp.arange(REQS, dtype=jnp.int32)
    is_owner = owner_slot[:, None] == slot_ids[None, :]
    inverse = lax.optimization_barrier(jnp.sum(jnp.where(is_owner, slot_ids[:, None], 0), axis=0)).astype(jnp.int32)

    def per_slot(slot):
        request = inverse[slot]
        first_row = (request * GROUP).astype(jnp.int32)
        query_rows = lax.dynamic_slice_in_dim(query_all, first_row, GROUP, 0).reshape(GROUP, HEADS, HEAD).astype(jnp.float32)
        new_k = lax.dynamic_slice_in_dim(keys_all, first_row, GROUP, 0)
        new_v = lax.dynamic_slice_in_dim(values_all, first_row, GROUP, 0)
        key_rows = jnp.concatenate([cache_keys[slot], new_k], axis=0).reshape(CACHE + GROUP, HEADS, HEAD).astype(jnp.float32)
        value_rows = jnp.concatenate([cache_values[slot], new_v], axis=0).reshape(CACHE + GROUP, HEADS, HEAD).astype(jnp.float32)
        length = cache_lengths[request]
        positions = jnp.arange(CACHE + GROUP, dtype=jnp.int32)[None, :]
        query_pos = jnp.arange(GROUP, dtype=jnp.int32)[:, None]
        is_valid = jnp.where(positions < CACHE, positions < length, positions - CACHE <= query_pos)
        scores = jnp.einsum('qhd,khd->hqk', query_rows, key_rows)
        masked = jnp.where(is_valid[None], scores, -jnp.inf)
        row_max = lax.optimization_barrier(jnp.max(masked, axis=-1))
        probs = jnp.where(is_valid[None], jnp.exp(scores - row_max[..., None]), 0.0)
        total = lax.optimization_barrier(jnp.sum(probs, axis=-1))
        rounded = probs.astype(jnp.bfloat16).astype(jnp.float32)
        attended = jnp.einsum('hqk,khd->hqd', rounded, value_rows) / total[..., None]
        return attended.transpose(1, 0, 2).reshape(GROUP, HD).astype(jnp.bfloat16)
    attended_all = lax.map(per_slot, slot_ids)
    new_keys = jnp.take(keys_all.reshape(REQS, GROUP, HD), inverse, axis=0)
    new_values = jnp.take(values_all.reshape(REQS, GROUP, HD), inverse, axis=0)
    ordered = jnp.take(attended_all, owner_slot, axis=0).reshape(TOKENS, HD)
    projected = jnp.dot(ordered, w_out, preferred_element_type=jnp.float32)
    hidden_out = (projected + bias_out + inputs).astype(jnp.bfloat16)
    return (hidden_out, new_keys, new_values)
```

```python
import functools

import jax
import jax.numpy as jnp
from jax import lax
from jax.experimental import pallas as pl
from jax.experimental.pallas import tpu as pltpu
from jax.sharding import PartitionSpec as P

HEAD = 128
F32 = jnp.float32
BF16 = jnp.bfloat16


def normalize(inputs, gain, bias):
    row_mean = jnp.mean(inputs, axis=-1, keepdims=True)
    centered = inputs - row_mean
    row_var = jnp.mean(centered * centered, axis=-1, keepdims=True)
    return centered * lax.rsqrt(row_var + 1e-05) * gain + bias


def swap(value, axis, mask, size):
    return lax.ppermute(value, axis, [(i, i ^ mask) for i in range(size)])


def attend_kernel(length_ref, q_ref, k_ref, v_ref, nk_ref, nv_ref, o_ref, m_ref, l_ref, acc_ref, *, key_len):
    length = length_ref[0]
    q = q_ref[...]
    group = q.shape[0]

    def scores_of(keys):
        return lax.dot_general(q, keys, (((1,), (1,)), ((), ())), preferred_element_type=F32)

    def lane_sum(probs):
        total = probs[:, :HEAD]
        for at in range(HEAD, probs.shape[1], HEAD):
            total = total + probs[:, at : at + HEAD]
        return total

    def visit(scores, values):
        old = m_ref[...]
        new = jnp.maximum(old, jnp.max(scores, axis=1, keepdims=True))
        factor = jnp.exp(old - new)
        probs = jnp.exp(scores - new)
        m_ref[...] = new
        l_ref[...] = l_ref[...] * factor + lane_sum(probs)
        acc_ref[...] = acc_ref[...] * factor + jnp.dot(probs.astype(BF16), values, preferred_element_type=F32)

    rows = lax.broadcasted_iota(jnp.int32, (group, group), 0)
    cols = lax.broadcasted_iota(jnp.int32, (group, group), 1)
    scores = jnp.where(cols <= rows, scores_of(nk_ref[...]), -1e30)
    new = jnp.max(scores, axis=1, keepdims=True)
    probs = jnp.exp(scores - new)
    m_ref[...] = new
    l_ref[...] = lane_sum(probs)
    acc_ref[...] = jnp.dot(probs.astype(BF16), nv_ref[...], preferred_element_type=F32)

    full = length // key_len

    def step(index, carry):
        at = pl.multiple_of(index * key_len, key_len)
        visit(scores_of(k_ref[0, pl.ds(at, key_len), :]), v_ref[0, pl.ds(at, key_len), :])
        return carry

    lax.fori_loop(0, full, step, 0)

    @pl.when(full * key_len < length)
    def _():
        at = pl.multiple_of(full * key_len, key_len)
        scores = scores_of(k_ref[0, pl.ds(at, key_len), :])
        positions = at + lax.broadcasted_iota(jnp.int32, (1, key_len), 1)
        visit(jnp.where(positions < length, scores, -1e30), v_ref[0, pl.ds(at, key_len), :])

    total = jnp.sum(l_ref[...], axis=1, keepdims=True)
    o_ref[...] = (acc_ref[...] / total).astype(BF16)


def attend(length, q, new_k, new_v, cache_k, cache_v, head_of):
    group, width = q.shape
    heads = width // HEAD
    cache_len = cache_k.shape[1]
    key_len = min(1024, cache_len)
    own = pl.BlockSpec((group, HEAD), lambda i, length: (0, i))
    cached = pl.BlockSpec((1, cache_len, HEAD), lambda i, length: (0, 0, head_of(i)))
    return pl.pallas_call(
        functools.partial(attend_kernel, key_len=key_len),
        out_shape=jax.ShapeDtypeStruct((group, width), BF16),
        grid_spec=pltpu.PrefetchScalarGridSpec(
            num_scalar_prefetch=1,
            grid=(heads,),
            in_specs=[own, cached, cached, own, own],
            out_specs=own,
            scratch_shapes=[
                pltpu.VMEM((group, 1), F32),
                pltpu.VMEM((group, HEAD), F32),
                pltpu.VMEM((group, HEAD), F32),
            ],
        ),
        compiler_params=pltpu.CompilerParams(vmem_limit_bytes=24 * 1024 * 1024),
        cost_estimate=pl.CostEstimate(
            flops=8 * group * (cache_len + group) * HEAD * heads,
            bytes_accessed=4 * (cache_len + 2 * group) * width,
            transcendentals=group * (cache_len + group) * heads,
        ),
    )(length, q, cache_k, cache_v, new_k, new_v)


def local(
    rows_n,
    cols_n,
    hidden_in,
    norm_gain,
    norm_bias,
    w_query,
    w_keyval,
    bias_query,
    bias_keyval,
    cache_keys,
    cache_values,
    cache_lengths,
    owner_slot,
    w_out,
    bias_out,
):
    row = lax.axis_index("row")
    col = lax.axis_index("col")
    core = row & 1
    group_len, width = hidden_in.shape
    slice_len, head_cols = w_query.shape
    heads = head_cols // HEAD
    half = heads // 2
    pairs = rows_n // 2
    row_bits = rows_n.bit_length() - 1
    col_bits = cols_n.bit_length() - 1
    q_scale = HEAD ** (-0.5)
    slot_ids = jnp.arange(rows_n, dtype=jnp.int32)
    is_owner = owner_slot[:, None] == slot_ids[None, :]
    inverse = jnp.sum(jnp.where(is_owner, slot_ids[:, None], 0), axis=0).astype(jnp.int32)
    length = cache_lengths[inverse[row]].reshape(1).astype(jnp.int32)

    stacked = jnp.concatenate([w_query[:, None, :], w_keyval], axis=1)
    stacked = stacked.reshape(slice_len, 3, 2, half, HEAD).transpose(2, 0, 3, 1, 4).reshape(2, slice_len, half * 3 * HEAD)
    kept = lax.dynamic_index_in_dim(stacked, core, 0, keepdims=False)
    given = lax.dynamic_index_in_dim(stacked, 1 - core, 0, keepdims=False)
    taken = swap(given, "row", 1, rows_n)
    first = jnp.where(core == 0, kept, taken)
    second = jnp.where(core == 0, taken, kept)
    weights = jnp.concatenate([first, second], axis=0)

    inputs = hidden_in.astype(F32)
    normed = normalize(inputs, norm_gain, norm_bias).astype(BF16)

    pair_len = 2 * slice_len
    pair = row // 2
    blocks = [None] * rows_n
    for offset in range(pairs):
        piece = lax.dynamic_slice_in_dim(normed, (pair ^ offset) * pair_len, pair_len, 1)
        if offset:
            piece = swap(piece, "row", 2 * offset, rows_n)
        blocks[2 * offset] = piece
        blocks[2 * offset + 1] = swap(piece, "row", 1, rows_n)

    products = []
    for offset in range(pairs):
        tokens = jnp.concatenate(blocks[2 * offset : 2 * offset + 2], axis=0)
        products.append(jnp.dot(tokens, weights, preferred_element_type=F32).astype(BF16))
    products = jnp.concatenate(products, axis=0).reshape(rows_n, group_len, half, 3 * HEAD)

    bias = jnp.concatenate([bias_query[None], bias_keyval], axis=0).reshape(3, 2, half, HEAD).transpose(1, 2, 0, 3)
    bias = lax.dynamic_index_in_dim(bias, core, 0, keepdims=False).reshape(half, 3 * HEAD)
    scale = jnp.concatenate([jnp.full((HEAD,), q_scale, F32), jnp.ones((2 * HEAD,), F32)])

    def to_slots(first_head, last_head, order):
        held = {
            e: lax.dynamic_index_in_dim(products[:, :, first_head:last_head], inverse[row ^ e] ^ row, 0, keepdims=False)
            for e in range(rows_n)
        }
        held = {e: v.reshape(group_len, -1) for e, v in held.items()}
        total = {e: v.astype(F32) for e, v in held.items()}
        left = list(range(rows_n))
        for bit in order:
            mask = 1 << bit
            out = [e for e in left if e & mask]
            left = [e for e in left if not e & mask]
            sent = jnp.stack([total[e].astype(BF16) for e in out])
            came = swap(sent, "row", mask, rows_n)
            for at, e in enumerate(left):
                total[e] = total[e] + came[at].astype(F32)
        count = last_head - first_head
        b = bias[first_head:last_head].reshape(-1)
        s = jnp.tile(scale, count)
        done = [((total[e] + b) * s).astype(BF16) for e in (0, 1)]
        other = swap(done[1], "row", 1, rows_n)
        lo = jnp.where(core == 0, done[0], other)
        hi = jnp.where(core == 0, other, done[0])
        return jnp.stack([lo, hi]).reshape(2, group_len, count, 3, HEAD)

    pair_bits = list(range(1, row_bits))
    groups = 3 if half % 3 == 0 else 1
    per_group = half // groups
    key_parts, value_parts, gathered = [], [], []
    for g in range(groups):
        base = g * per_group
        cuts = [base, base + per_group // 2, base + per_group] if per_group > 1 else [base, base + 1]
        parts = []
        for at in range(len(cuts) - 1):
            shift = at % max(1, len(pair_bits))
            parts.append(to_slots(cuts[at], cuts[at + 1], pair_bits[shift:] + pair_bits[:shift]))
        mine = jnp.concatenate(parts, axis=2)
        q, k, v = (mine[:, :, :, i].transpose(1, 0, 2, 3).reshape(group_len, 2 * per_group * HEAD) for i in range(3))
        key_parts.append(k.reshape(group_len, 2, per_group * HEAD))
        value_parts.append(v.reshape(group_len, 2, per_group * HEAD))
        attended = attend(
            length,
            q,
            k,
            v,
            cache_keys,
            cache_values,
            lambda i, base=base: (i // per_group) * half + base + i % per_group,
        )
        every = [None] * rows_n
        for offset in range(pairs):
            piece = swap(attended, "row", 2 * offset, rows_n) if offset else attended
            every[2 * offset] = piece
            every[2 * offset + 1] = swap(piece, "row", 1, rows_n)
        gathered.append(jnp.stack(every).reshape(rows_n, group_len, 2, per_group * HEAD))

    new_k = jnp.concatenate(key_parts, axis=2).reshape(1, group_len, head_cols)
    new_v = jnp.concatenate(value_parts, axis=2).reshape(1, group_len, head_cols)
    heads_all = jnp.concatenate(gathered, axis=3).reshape(rows_n, group_len, head_cols)

    places = owner_slot[row ^ slot_ids] ^ row
    shift = row_bits - col_bits
    chunks = 2
    chunk_len = group_len // chunks
    results = []
    for c in range(chunks):
        tokens = jnp.concatenate(
            [
                lax.dynamic_slice(heads_all, (places[e], c * chunk_len, 0), (1, chunk_len, head_cols))[0]
                for e in range(rows_n)
            ],
            axis=0,
        )
        partial = jnp.dot(tokens, w_out, preferred_element_type=F32).astype(BF16)
        held = {(e, 0): partial[e * chunk_len : (e + 1) * chunk_len] for e in range(rows_n)}
        for bit in range(row_bits):
            mask = 1 << bit
            out = [key for key in sorted(held) if key[0] & mask]
            keep = [key for key in sorted(held) if not key[0] & mask]
            came = swap(jnp.stack([held[key] for key in out]), "row", mask, rows_n)
            after = {key: held[key] for key in keep}
            for at, (e, j) in enumerate(out):
                after[(e ^ mask, j ^ mask)] = came[at]
            held = after
            if bit >= shift:
                cmask = 1 << (bit - shift)
                flip = ((row >> bit) ^ (col >> (bit - shift))) & 1
                keys = [key for key in sorted(held) if not key[1] & mask]
                low = jnp.stack([held[key] for key in keys])
                high = jnp.stack([held[(e, j ^ mask)] for e, j in keys])
                keep_part = jnp.where(flip == 0, low, high)
                send_part = jnp.where(flip == 0, high, low)
                came = swap(send_part, "col", cmask, cols_n)
                summed = keep_part.astype(F32) + came.astype(F32)
                last = bit == row_bits - 1
                summed = summed if last else summed.astype(BF16)
                held = {key: summed[at] for at, key in enumerate(keys)}
        count = 1 << shift
        stacked_out = jnp.stack([held[(0, j)] for j in range(count)])
        low_bits = row & (count - 1)
        ordered = jnp.concatenate(
            [lax.dynamic_index_in_dim(stacked_out, low_bits ^ j, 0, keepdims=False) for j in range(count)], axis=1
        )
        results.append(ordered)
    summed_out = jnp.concatenate(results, axis=0)
    out_cols = summed_out.shape[1]
    residual = lax.dynamic_slice_in_dim(hidden_in, col * out_cols, out_cols, 1).astype(F32)
    hidden_out = (summed_out.astype(F32) + bias_out + residual).astype(BF16)
    return hidden_out, new_k, new_v


def solution(mesh):
    placed = (
        P("row", None),
        P(),
        P(),
        P("row", "col"),
        P("row", None, "col"),
        P("col"),
        P(None, "col"),
        P("row", None, "col"),
        P("row", None, "col"),
        P(),
        P(),
        P("col", "row"),
        P("col"),
    )
    return jax.shard_map(
        functools.partial(local, mesh.shape["row"], mesh.shape["col"]),
        mesh=mesh,
        in_specs=placed,
        out_specs=(P("row", "col"), P("row", None, "col"), P("row", None, "col")),
        check_vma=False,
    )
```

```python
import functools

import jax
import jax.numpy as jnp
from jax import lax
from jax.experimental import pallas as pl
from jax.experimental.pallas import tpu as pltpu
from jax.sharding import PartitionSpec as P

HEAD = 128
F32 = jnp.float32
BF16 = jnp.bfloat16


def normalize(inputs, gain, bias):
    row_mean = jnp.mean(inputs, axis=-1, keepdims=True)
    centered = inputs - row_mean
    row_var = jnp.mean(centered * centered, axis=-1, keepdims=True)
    return centered * lax.rsqrt(row_var + 1e-05) * gain + bias


def swap(value, axis, mask, size):
    return lax.ppermute(value, axis, [(i, i ^ mask) for i in range(size)])


def gather_block(table, places, dst, sem):
    for at, place in enumerate(places):

        @pl.when(table == at)
        def _(place=place):
            pltpu.make_async_copy(place, dst, sem).start()


def project_kernel(meta_ref, *refs, blocks, group, orders):
    x_refs, (wq_ref, wkv_ref, taken_ref) = refs[:blocks], refs[blocks : blocks + 3]
    out_refs, (x_buf, w_buf, x_sem, w_sem) = refs[blocks + 3 : -4], refs[-4:]
    core = meta_ref[0]
    slice_len, head_cols = wq_ref.shape
    half_cols = head_cols // 2
    cols = w_buf.shape[1] // 3
    heads = cols // HEAD
    for kind in range(3):
        source, first = (wq_ref, 0) if kind == 0 else (wkv_ref, (kind - 1) * head_cols)
        at = pl.multiple_of(first + core * half_cols + group * cols, HEAD)
        own = pl.ds(pl.multiple_of(core * slice_len, 16), slice_len)
        other = pl.ds(pl.multiple_of((1 - core) * slice_len, 16), slice_len)
        there = pl.ds(kind * cols, cols)
        pltpu.make_async_copy(source.at[:, pl.ds(at, cols)], w_buf.at[own, there], w_sem.at[2 * kind]).start()
        pltpu.make_async_copy(
            taken_ref.at[:, pl.ds(kind * half_cols + group * cols, cols)], w_buf.at[other, there], w_sem.at[2 * kind + 1]
        ).start()
    pairs = sorted(range(0, blocks, 2), key=lambda e: -sum(bool(e >> order[0] & 1) for order in orders))
    for e in pairs:
        for c in range(2):
            gather_block(meta_ref[1 + e + c], x_refs, x_buf.at[e + c], x_sem.at[e + c])
    for at in range(6):
        half = pl.ds(0, slice_len)
        pltpu.make_async_copy(
            taken_ref.at[:, pl.ds(0, cols)], w_buf.at[half, pl.ds(0, cols)], w_sem.at[at]
        ).wait()
    group_len = x_buf.shape[1]
    for e in pairs:
        for c in range(2):
            pltpu.make_async_copy(x_refs[0], x_buf.at[e + c], x_sem.at[e + c]).wait()
        tokens = x_buf[e : e + 2].reshape(2 * group_len, x_buf.shape[2])
        product = jnp.dot(tokens, w_buf[...], preferred_element_type=F32).astype(BF16)
        first = 0
        for p, order in enumerate(orders):
            keep_ref, send_ref = out_refs[2 * p], out_refs[2 * p + 1]
            count = keep_ref.shape[2] // (3 * HEAD)
            ranked = slots_in(blocks, order)
            for c in range(2):
                place = ranked.index(e + c)
                ref = keep_ref if place < blocks // 2 else send_ref
                for h in range(count):
                    for kind in range(3):
                        at = kind * cols + (first + h) * HEAD
                        ref[place % (blocks // 2), :, pl.ds((3 * h + kind) * HEAD, HEAD)] = product[
                            c * group_len : (c + 1) * group_len, at : at + HEAD
                        ]
            first += count


def slots_in(blocks, order):
    return sorted(range(blocks), key=lambda e: [e >> bit & 1 for bit in order] + [e & 1])


def project(meta, x_blocks, w_query, w_keyval, taken, group, per_group, orders, counts):
    blocks = len(x_blocks)
    group_len, depth = x_blocks[0].shape
    hbm = pl.BlockSpec(memory_space=pltpu.HBM)
    out_shape = []
    for count in counts:
        out_shape += [jax.ShapeDtypeStruct((blocks // 2, group_len, count * 3 * HEAD), BF16)] * 2
    cols = per_group * 3 * HEAD
    return pl.pallas_call(
        functools.partial(project_kernel, blocks=blocks, group=group, orders=orders),
        out_shape=out_shape,
        in_specs=[pl.BlockSpec(memory_space=pltpu.SMEM)] + [hbm] * (blocks + 3),
        out_specs=[pl.BlockSpec(memory_space=pltpu.VMEM)] * len(out_shape),
        scratch_shapes=[
            pltpu.VMEM((blocks, group_len, depth), BF16),
            pltpu.VMEM((depth, cols), BF16),
            pltpu.SemaphoreType.DMA((blocks,)),
            pltpu.SemaphoreType.DMA((6,)),
        ],
        compiler_params=pltpu.CompilerParams(vmem_limit_bytes=48 * 1024 * 1024),
        cost_estimate=pl.CostEstimate(
            flops=2 * blocks * group_len * depth * cols,
            bytes_accessed=2 * (blocks * group_len * (depth + cols) + depth * cols),
            transcendentals=0,
        ),
    )(meta, *x_blocks, w_query, w_keyval, taken)


def attend_kernel(meta_ref, qkv_ref, k_ref, v_ref, o_ref, nk_ref, nv_ref, *, key_len):
    length = meta_ref[0]
    qkv = qkv_ref[0]
    q, new_k, new_v = qkv[:, :HEAD], qkv[:, HEAD : 2 * HEAD], qkv[:, 2 * HEAD :]
    nk_ref[...] = new_k
    nv_ref[...] = new_v
    group = q.shape[0]
    cache_len = k_ref.shape[1]

    def scores_of(at):
        keys = k_ref[0, at : at + key_len, :]
        scores = lax.dot_general(q, keys, (((1,), (1,)), ((), ())), preferred_element_type=F32)
        positions = at + lax.broadcasted_iota(jnp.int32, (1, key_len), 1)
        return jnp.where(positions < length, scores, -1e30)

    def lane_sum(probs):
        total = probs[:, :HEAD]
        for at in range(HEAD, probs.shape[1], HEAD):
            total = total + probs[:, at : at + HEAD]
        return total

    rows = lax.broadcasted_iota(jnp.int32, (group, group), 0)
    cols = lax.broadcasted_iota(jnp.int32, (group, group), 1)
    scores = lax.dot_general(q, new_k, (((1,), (1,)), ((), ())), preferred_element_type=F32)
    scores = jnp.where(cols <= rows, scores, -1e30)
    following = scores_of(0)
    row_max = jnp.max(scores, axis=1, keepdims=True)
    probs = jnp.exp(scores - row_max)
    row_sum = lane_sum(probs)
    weighted = jnp.dot(probs.astype(BF16), new_v, preferred_element_type=F32)
    for at in range(0, cache_len, key_len):
        scores = following
        if at + key_len < cache_len:
            following = scores_of(at + key_len)
        new_max = jnp.maximum(row_max, jnp.max(scores, axis=1, keepdims=True))
        factor = jnp.exp(row_max - new_max)
        probs = jnp.exp(scores - new_max)
        row_max = new_max
        row_sum = row_sum * factor + lane_sum(probs)
        values = v_ref[0, at : at + key_len, :]
        weighted = weighted * factor + jnp.dot(probs.astype(BF16), values, preferred_element_type=F32)
    total = jnp.sum(row_sum, axis=1, keepdims=True)
    o_ref[...] = (weighted / total).astype(BF16)


def attend(meta, qkv, cache_k, cache_v, base, half):
    heads, group, _ = qkv.shape
    count = heads // 2
    cache_len = cache_k.shape[1]
    key_len = min(512, cache_len)

    def side(i, meta):
        return (i // count) ^ meta[1]

    cached = pl.BlockSpec((1, cache_len, HEAD), lambda i, meta: (0, 0, side(i, meta) * half + base + i % count))
    placed = pl.BlockSpec((group, HEAD), lambda i, meta: (0, side(i, meta) * count + i % count))
    return pl.pallas_call(
        functools.partial(attend_kernel, key_len=key_len),
        out_shape=[jax.ShapeDtypeStruct((group, heads * HEAD), BF16)] * 3,
        grid_spec=pltpu.PrefetchScalarGridSpec(
            num_scalar_prefetch=1,
            grid=(heads,),
            in_specs=[pl.BlockSpec((1, group, 3 * HEAD), lambda i, meta: (i, 0, 0)), cached, cached],
            out_specs=[placed] * 3,
        ),
        compiler_params=pltpu.CompilerParams(vmem_limit_bytes=56 * 1024 * 1024),
        cost_estimate=pl.CostEstimate(
            flops=8 * group * (cache_len + group) * HEAD * heads,
            bytes_accessed=4 * (cache_len + 2 * group) * heads * HEAD,
            transcendentals=group * (cache_len + group) * heads,
        ),
    )(meta, qkv, cache_k, cache_v)


def output_kernel(meta_ref, *refs, blocks, groups, first):
    a_refs = [refs[g * blocks : (g + 1) * blocks] for g in range(groups)]
    w_ref = refs[groups * blocks]
    out_refs, (buf, sem) = refs[groups * blocks + 1 : -2], refs[-2:]
    _, chunk, head_cols = buf.shape
    half = head_cols // 2
    cols = half // groups
    ranked = output_order(blocks)
    for at, e in enumerate(ranked):
        for i in range(blocks):

            @pl.when(meta_ref[e] == i)
            def _(at=at, i=i):
                for g in range(groups):
                    for side in range(2):
                        pltpu.make_async_copy(
                            a_refs[g][i].at[pl.ds(first, chunk), pl.ds(side * cols, cols)],
                            buf.at[at, :, pl.ds(side * half + g * cols, cols)],
                            sem.at[at],
                        ).start()

    quarter = blocks // 4
    for part in range(4):
        for at in range(part * quarter, (part + 1) * quarter):
            pltpu.make_async_copy(buf.at[at], buf.at[at], sem.at[at]).wait()
        tokens = buf[part * quarter : (part + 1) * quarter].reshape(quarter * chunk, head_cols)
        product = jnp.dot(tokens, w_ref[...], preferred_element_type=F32).astype(BF16)
        out_refs[part][...] = product.reshape(out_refs[part].shape)


def output_order(blocks):
    bits = blocks.bit_length() - 1
    return sorted(range(blocks), key=lambda e: [1 - (e & 1), e >> 1 & 1] + [e >> bit & 1 for bit in range(2, bits)])


def output(meta, gathered, w_out, first, chunk):
    groups, blocks = len(gathered), len(gathered[0])
    head_cols, out_cols = w_out.shape
    hbm = pl.BlockSpec(memory_space=pltpu.HBM)
    vmem = pl.BlockSpec(memory_space=pltpu.VMEM)
    return pl.pallas_call(
        functools.partial(output_kernel, blocks=blocks, groups=groups, first=first),
        out_shape=[jax.ShapeDtypeStruct((blocks // 4, chunk, out_cols), BF16)] * 4,
        in_specs=[pl.BlockSpec(memory_space=pltpu.SMEM)] + [hbm] * (groups * blocks) + [vmem],
        out_specs=[vmem] * 4,
        scratch_shapes=[pltpu.VMEM((blocks, chunk, head_cols), BF16), pltpu.SemaphoreType.DMA((blocks,))],
        compiler_params=pltpu.CompilerParams(vmem_limit_bytes=40 * 1024 * 1024),
        cost_estimate=pl.CostEstimate(
            flops=2 * blocks * chunk * head_cols * out_cols,
            bytes_accessed=2 * (blocks * chunk * (head_cols + out_cols) + head_cols * out_cols),
            transcendentals=0,
        ),
    )(meta, *[a for part in gathered for a in part], w_out)


def local(
    rows_n,
    cols_n,
    hidden_in,
    norm_gain,
    norm_bias,
    w_query,
    w_keyval,
    bias_query,
    bias_keyval,
    cache_keys,
    cache_values,
    cache_lengths,
    owner_slot,
    w_out,
    bias_out,
):
    row = lax.axis_index("row")
    col = lax.axis_index("col")
    core = row & 1
    group_len, width = hidden_in.shape
    slice_len, head_cols = w_query.shape
    half = head_cols // HEAD // 2
    half_cols = head_cols // 2
    pairs = rows_n // 2
    row_bits = rows_n.bit_length() - 1
    col_bits = cols_n.bit_length() - 1
    q_scale = HEAD ** (-0.5)
    slot_ids = jnp.arange(rows_n, dtype=jnp.int32)
    is_owner = owner_slot[:, None] == slot_ids[None, :]
    inverse = jnp.sum(jnp.where(is_owner, slot_ids[:, None], 0), axis=0).astype(jnp.int32)

    inputs = hidden_in.astype(F32)
    normed = normalize(inputs, norm_gain, norm_bias).astype(BF16)

    pair_len = 2 * slice_len
    pair = row // 2
    pieces = [lax.dynamic_slice_in_dim(normed, (pair ^ offset) * pair_len, pair_len, 1) for offset in range(pairs)]
    *pieces, w_query, w_keyval = lax.optimization_barrier((*pieces, w_query, w_keyval))
    x_blocks = [None] * rows_n
    for offset in reversed(range(pairs)):
        piece = swap(pieces[offset], "row", 2 * offset, rows_n) if offset else pieces[0]
        x_blocks[2 * offset] = piece
        x_blocks[2 * offset + 1] = swap(piece, "row", 1, rows_n)

    w_flat = w_keyval.reshape(slice_len, 2 * head_cols)
    given = jnp.concatenate(
        [
            lax.dynamic_slice_in_dim(source, first + (1 - core) * half_cols, half_cols, 1)
            for source, first in ((w_query, 0), (w_flat, 0), (w_flat, head_cols))
        ],
        axis=1,
    )
    taken = swap(given, "row", 1, rows_n)

    bias = jnp.concatenate([bias_query[None], bias_keyval], axis=0).reshape(3, 2, half, HEAD).transpose(1, 2, 0, 3)
    bias = lax.dynamic_index_in_dim(bias, core, 0, keepdims=False).reshape(half, 3 * HEAD)
    scale = jnp.concatenate([jnp.full((HEAD,), q_scale, F32), jnp.ones((2 * HEAD,), F32)])

    groups = 3 if half % 3 == 0 else 1
    per_group = half // groups
    counts = [per_group // 2, per_group - per_group // 2] if per_group > 1 else [1]
    pair_bits = list(range(1, row_bits))
    orders = [pair_bits[at % len(pair_bits) :] + pair_bits[: at % len(pair_bits)] for at in range(len(counts))]
    project_meta = jnp.concatenate([core[None], inverse[row ^ slot_ids] ^ row]).astype(jnp.int32)
    attend_meta = jnp.stack([cache_lengths[inverse[row]], core]).astype(jnp.int32)

    projected = [
        project(project_meta, x_blocks, w_query, w_flat, taken, g, per_group, orders, counts) for g in range(groups)
    ]
    key_parts, value_parts, gathered = [], [], []
    for g in range(groups):
        base = g * per_group
        own, other = [], []
        for p, order in enumerate(orders):
            keep, send = projected[g][2 * p : 2 * p + 2]
            terms = [keep]
            for bit in order:
                came = swap(send, "row", 1 << bit, rows_n)
                terms = [t[: came.shape[0]] for t in terms] + [came]
                left = came.shape[0] // 2
                if left > 1:
                    send = sum(t[left:].astype(F32) for t in terms).astype(BF16)
            at = base + sum(counts[:p])
            b = bias[at : at + counts[p]].reshape(-1)
            s = jnp.tile(scale, counts[p])
            mine, theirs = (((sum(t[e].astype(F32) for t in terms) + b) * s).astype(BF16) for e in (0, 1))
            came = swap(theirs, "row", 1, rows_n)
            own += [mine[:, 3 * HEAD * h : 3 * HEAD * (h + 1)] for h in range(counts[p])]
            other += [came[:, 3 * HEAD * h : 3 * HEAD * (h + 1)] for h in range(counts[p])]
        attended, new_k, new_v = attend(attend_meta, jnp.stack(own + other), cache_keys, cache_values, base, half)
        key_parts.append(new_k)
        value_parts.append(new_v)
        every = [None] * rows_n
        for offset in reversed(range(pairs)):
            piece = swap(attended, "row", 2 * offset, rows_n) if offset else attended
            every[2 * offset] = piece
            every[2 * offset + 1] = swap(piece, "row", 1, rows_n)
        gathered.append(every)

    cols = per_group * HEAD
    new_k, new_v = (
        jnp.concatenate([p[:, side * cols : (side + 1) * cols] for side in range(2) for p in parts], axis=1)[None]
        for parts in (key_parts, value_parts)
    )

    places = (owner_slot[row ^ slot_ids] ^ row).astype(jnp.int32)
    shift = row_bits - col_bits
    low_bits = row & ((1 << shift) - 1)
    out_cols = width // cols_n
    residual = lax.dynamic_slice_in_dim(hidden_in, col * out_cols, out_cols, 1).astype(F32) + bias_out
    chunks = 4
    chunk = group_len // chunks
    results = []
    for c in range(chunks):
        send_a, send_b, keep_a, keep_b = output(places, gathered, w_out, c * chunk, chunk)
        held = {0: [keep_a, keep_b], 1: [swap(send_a, "row", 1, rows_n), swap(send_b, "row", 1, rows_n)]}
        for bit in range(1, row_bits):
            mask = 1 << bit
            after = {}
            for j, parts in held.items():
                keep, send = parts if bit == 1 else (parts[: parts.shape[0] // 2], parts[parts.shape[0] // 2 :])
                after[j], after[j | mask] = keep, swap(send, "row", mask, rows_n)
            held = after
            if bit >= shift:
                cmask = 1 << (bit - shift)
                flip = ((row >> bit) ^ (col >> (bit - shift))) & 1
                after = {}
                for j in sorted(held):
                    if j & mask:
                        continue
                    low, high = held[j], held[j | mask]
                    came = swap(jnp.where(flip == 0, high, low), "col", cmask, cols_n)
                    total = jnp.where(flip == 0, low, high).astype(F32) + came.astype(F32)
                    after[j] = total if bit == row_bits - 1 else total.astype(BF16)
                held = after
        count = 1 << shift
        stacked = jnp.concatenate([held[j] for j in range(count)], axis=0)
        results.append(
            jnp.concatenate(
                [lax.dynamic_index_in_dim(stacked, low_bits ^ j, 0, keepdims=False) for j in range(count)], axis=1
            )
        )
    hidden_out = (jnp.concatenate(results, axis=0) + residual).astype(BF16)
    return hidden_out, new_k, new_v


def solution(mesh):
    placed = (
        P("row", None),
        P(),
        P(),
        P("row", "col"),
        P("row", None, "col"),
        P("col"),
        P(None, "col"),
        P("row", None, "col"),
        P("row", None, "col"),
        P(),
        P(),
        P("col", "row"),
        P("col"),
    )
    return jax.shard_map(
        functools.partial(local, mesh.shape["row"], mesh.shape["col"]),
        mesh=mesh,
        in_specs=placed,
        out_specs=(P("row", "col"), P("row", None, "col"), P("row", None, "col")),
        check_vma=False,
    )
```

```python
import functools

import jax
import jax.numpy as jnp
from jax import lax
from jax.experimental import pallas as pl
from jax.experimental.pallas import tpu as pltpu
from jax.sharding import PartitionSpec as P

HEAD = 128
F32 = jnp.float32
BF16 = jnp.bfloat16


def normalize_kernel(meta_ref, hidden_ref, gain_ref, bias_ref, *out_refs):
    *piece_refs, core_ref = out_refs
    core_ref[0] = meta_ref[1]
    width = hidden_ref.shape[1]
    length = piece_refs[0].shape[1]
    rows = hidden_ref[...].astype(F32)
    mean = jnp.sum(rows, axis=1, keepdims=True) / width
    centered = rows - mean
    var = jnp.sum(centered * centered, axis=1, keepdims=True) / width
    factor = lax.rsqrt(var + 1e-05)
    for d, ref in enumerate(piece_refs):
        part = pl.ds(pl.multiple_of((meta_ref[0] ^ d) * length, HEAD), length)
        ref[...] = ((hidden_ref[:, part].astype(F32) - mean) * factor * gain_ref[:, part] + bias_ref[:, part]).astype(BF16)


def normalize(meta, hidden, gain, bias, pairs):
    rows, width = hidden.shape
    step = 32
    whole = pl.BlockSpec((1, width), lambda i, meta: (0, 0))
    *pieces, core = pl.pallas_call(
        normalize_kernel,
        out_shape=[jax.ShapeDtypeStruct((rows, width // pairs), BF16)] * pairs + [jax.ShapeDtypeStruct((1,), jnp.int32)],
        grid_spec=pltpu.PrefetchScalarGridSpec(
            num_scalar_prefetch=1,
            grid=(rows // step,),
            in_specs=[pl.BlockSpec((step, width), lambda i, meta: (i, 0)), whole, whole],
            out_specs=[pl.BlockSpec((step, width // pairs), lambda i, meta: (i, 0))] * pairs
            + [pl.BlockSpec(memory_space=pltpu.SMEM)],
        ),
        compiler_params=pltpu.CompilerParams(vmem_limit_bytes=24 * 1024 * 1024),
        cost_estimate=pl.CostEstimate(flops=10 * rows * width, bytes_accessed=4 * rows * width, transcendentals=rows),
    )(meta, hidden, gain[None], bias[None])
    return pieces, core[0]


def swap(value, axis, mask, size):
    return lax.ppermute(value, axis, [(i, i ^ mask) for i in range(size)])


def gather_block(table, places, dst, sem):
    for at, place in enumerate(places):

        @pl.when(table == at)
        def _(place=place):
            pltpu.make_async_copy(place, dst, sem).start()


def project_kernel(meta_ref, *refs, blocks, group, orders):
    x_refs, (wq_ref, wkv_ref, taken_ref) = refs[:blocks], refs[blocks : blocks + 3]
    out_refs, (x_buf, w_buf, x_sem, w_sem) = refs[blocks + 3 : -4], refs[-4:]
    core = meta_ref[0]
    slice_len, head_cols = wq_ref.shape
    half_cols = head_cols // 2
    cols = w_buf.shape[1] // 3
    heads = cols // HEAD
    for kind in range(3):
        source, first = (wq_ref, core * half_cols) if kind == 0 else (wkv_ref, (kind - 1) * half_cols)
        at = pl.multiple_of(first + group * cols, HEAD)
        own = pl.ds(pl.multiple_of(core * slice_len, 16), slice_len)
        other = pl.ds(pl.multiple_of((1 - core) * slice_len, 16), slice_len)
        there = pl.ds(kind * cols, cols)
        pltpu.make_async_copy(source.at[:, pl.ds(at, cols)], w_buf.at[own, there], w_sem.at[2 * kind]).start()
        pltpu.make_async_copy(
            taken_ref.at[:, pl.ds(kind * half_cols + group * cols, cols)], w_buf.at[other, there], w_sem.at[2 * kind + 1]
        ).start()
    sequence = sorted(range(blocks), key=lambda e: -sum(bool(e >> order[0] & 1) for order in orders))
    for at, e in enumerate(sequence):
        gather_block(meta_ref[1 + e], x_refs, x_buf.at[at], x_sem.at[at])
    for at in range(6):
        half = pl.ds(0, slice_len)
        pltpu.make_async_copy(
            taken_ref.at[:, pl.ds(0, cols)], w_buf.at[half, pl.ds(0, cols)], w_sem.at[at]
        ).wait()
    group_len = x_buf.shape[1]
    batch = 4
    for start in range(0, blocks, batch):
        for at in range(start, start + batch):
            pltpu.make_async_copy(x_refs[0], x_buf.at[at], x_sem.at[at]).wait()
        tokens = x_buf[start : start + batch].reshape(batch * group_len, x_buf.shape[2])
        product = jnp.dot(tokens, w_buf[...], preferred_element_type=F32).astype(BF16)
        first = 0
        for p, order in enumerate(orders):
            keep_ref, send_ref = out_refs[2 * p], out_refs[2 * p + 1]
            count = keep_ref.shape[2] // (3 * HEAD)
            ranked = slots_in(blocks, order)
            for c in range(batch):
                place = ranked.index(sequence[start + c])
                ref = keep_ref if place < blocks // 2 else send_ref
                for h in range(count):
                    for kind in range(3):
                        at = kind * cols + (first + h) * HEAD
                        ref[place % (blocks // 2), :, pl.ds((3 * h + kind) * HEAD, HEAD)] = product[
                            c * group_len : (c + 1) * group_len, at : at + HEAD
                        ]
            first += count


def slots_in(blocks, order):
    return sorted(range(blocks), key=lambda e: [e >> bit & 1 for bit in order] + [e & 1])


def project(meta, x_blocks, w_query, w_keyval, taken, group, per_group, orders, counts):
    blocks = len(x_blocks)
    group_len, depth = x_blocks[0].shape
    hbm = pl.BlockSpec(memory_space=pltpu.HBM)
    out_shape = []
    for count in counts:
        out_shape += [jax.ShapeDtypeStruct((blocks // 2, group_len, count * 3 * HEAD), BF16)] * 2
    cols = per_group * 3 * HEAD
    return pl.pallas_call(
        functools.partial(project_kernel, blocks=blocks, group=group, orders=orders),
        out_shape=out_shape,
        in_specs=[pl.BlockSpec(memory_space=pltpu.SMEM)] + [hbm] * (blocks + 3),
        out_specs=[pl.BlockSpec(memory_space=pltpu.VMEM)] * len(out_shape),
        scratch_shapes=[
            pltpu.VMEM((blocks, group_len, depth), BF16),
            pltpu.VMEM((depth, cols), BF16),
            pltpu.SemaphoreType.DMA((blocks,)),
            pltpu.SemaphoreType.DMA((6,)),
        ],
        compiler_params=pltpu.CompilerParams(vmem_limit_bytes=48 * 1024 * 1024),
        cost_estimate=pl.CostEstimate(
            flops=2 * blocks * group_len * depth * cols,
            bytes_accessed=2 * (blocks * group_len * (depth + cols) + depth * cols),
            transcendentals=0,
        ),
    )(meta, *x_blocks, w_query, w_keyval, taken)


def forward_kernel(*refs, parts, terms, behind):
    out_refs = refs[parts * terms + behind :]
    for p in range(parts):
        mine = refs[p * terms : (p + 1) * terms]
        out_refs[p][...] = sum(ref[...].astype(F32) for ref in mine).astype(BF16)


def forward(terms, behind):
    left = min(t.shape[0] for t in terms[0]) // 2
    shapes = [(left, *ts[0].shape[1:]) for ts in terms]
    specs = [pl.BlockSpec(shape, lambda i: (1, 0, 0)) for shape, ts in zip(shapes, terms) for _ in ts]
    return pl.pallas_call(
        functools.partial(forward_kernel, parts=len(terms), terms=len(terms[0]), behind=len(behind)),
        grid=(1,),
        out_shape=[jax.ShapeDtypeStruct(shape, BF16) for shape in shapes],
        in_specs=specs + [pl.BlockSpec(memory_space=pltpu.HBM)] * len(behind),
        out_specs=[pl.BlockSpec(shape, lambda i: (0, 0, 0)) for shape in shapes],
        compiler_params=pltpu.CompilerParams(vmem_limit_bytes=24 * 1024 * 1024),
    )(*[t for ts in terms for t in ts], *behind)


def settle_kernel(bias_ref, scale_ref, *refs, parts, terms, behind):
    mine_ref, theirs_ref = refs[parts * terms + behind :]
    width = mine_ref.shape[2]
    head = 0
    for p in range(parts):
        for h in range(refs[p * terms].shape[2] // width):
            cols = pl.ds(h * width, width)
            for e, ref in enumerate((mine_ref, theirs_ref)):
                total = sum(t[e, :, cols].astype(F32) for t in refs[p * terms : (p + 1) * terms])
                ref[head] = ((total + bias_ref[head : head + 1, :]) * scale_ref[...]).astype(BF16)
            head += 1


def settle(terms, bias, scale, behind):
    heads, width = bias.shape
    rows = terms[0][0].shape[1]
    specs = [pl.BlockSpec((2, *t.shape[1:]), lambda i: (0, 0, 0)) for ts in terms for t in ts]
    whole = pl.BlockSpec((heads, rows, width), lambda i: (0, 0, 0))
    return pl.pallas_call(
        functools.partial(settle_kernel, parts=len(terms), terms=len(terms[0]), behind=len(behind)),
        grid=(1,),
        out_shape=[jax.ShapeDtypeStruct((heads, rows, width), BF16)] * 2,
        in_specs=[pl.BlockSpec((heads, width), lambda i: (0, 0)), pl.BlockSpec((1, width), lambda i: (0, 0))]
        + specs
        + [pl.BlockSpec(memory_space=pltpu.HBM)] * len(behind),
        out_specs=[whole, whole],
        compiler_params=pltpu.CompilerParams(vmem_limit_bytes=24 * 1024 * 1024),
    )(bias, scale, *[t for ts in terms for t in ts], *behind)


def attend_kernel(meta_ref, own_ref, other_ref, k_ref, v_ref, o_ref, nk_ref, nv_ref, *, key_len):
    length = meta_ref[0]
    qkv = jnp.where(pl.program_id(0) < pl.num_programs(0) // 2, own_ref[0], other_ref[0])
    q, new_k, new_v = qkv[:, :HEAD], qkv[:, HEAD : 2 * HEAD], qkv[:, 2 * HEAD :]
    nk_ref[...] = new_k
    nv_ref[...] = new_v
    group = q.shape[0]
    cache_len = k_ref.shape[1]

    def scores_of(at):
        keys = k_ref[0, at : at + key_len, :]
        scores = lax.dot_general(q, keys, (((1,), (1,)), ((), ())), preferred_element_type=F32)
        positions = at + lax.broadcasted_iota(jnp.int32, (1, key_len), 1)
        return jnp.where(positions < length, scores, -1e30)

    def lane_sum(probs):
        total = probs[:, :HEAD]
        for at in range(HEAD, probs.shape[1], HEAD):
            total = total + probs[:, at : at + HEAD]
        return total

    rows = lax.broadcasted_iota(jnp.int32, (group, group), 0)
    cols = lax.broadcasted_iota(jnp.int32, (group, group), 1)
    scores = lax.dot_general(q, new_k, (((1,), (1,)), ((), ())), preferred_element_type=F32)
    scores = jnp.where(cols <= rows, scores, -1e30)
    following = scores_of(0)
    row_max = jnp.max(scores, axis=1, keepdims=True)
    probs = jnp.exp(scores - row_max)
    row_sum = lane_sum(probs)
    weighted = jnp.dot(probs.astype(BF16), new_v, preferred_element_type=F32)
    for at in range(0, cache_len, key_len):
        scores = following
        if at + key_len < cache_len:
            following = scores_of(at + key_len)
        new_max = jnp.maximum(row_max, jnp.max(scores, axis=1, keepdims=True))
        factor = jnp.exp(row_max - new_max)
        probs = jnp.exp(scores - new_max)
        row_max = new_max
        row_sum = row_sum * factor + lane_sum(probs)
        values = v_ref[0, at : at + key_len, :]
        weighted = weighted * factor + jnp.dot(probs.astype(BF16), values, preferred_element_type=F32)
    total = jnp.sum(row_sum, axis=1, keepdims=True)
    o_ref[...] = (weighted / total).astype(BF16)


def attend(meta, own, other, cache_k, cache_v, base, half):
    count, group, width = own.shape
    heads = 2 * count
    cache_len = cache_k.shape[1]
    key_len = min(512, cache_len)

    def side(i, meta):
        return (i // count) ^ meta[1]

    cached = pl.BlockSpec((1, cache_len, HEAD), lambda i, meta: (0, 0, side(i, meta) * half + base + i % count))
    placed = pl.BlockSpec((group, HEAD), lambda i, meta: (0, side(i, meta) * count + i % count))
    return pl.pallas_call(
        functools.partial(attend_kernel, key_len=key_len),
        out_shape=[jax.ShapeDtypeStruct((group, heads * HEAD), BF16)] * 3,
        grid_spec=pltpu.PrefetchScalarGridSpec(
            num_scalar_prefetch=1,
            grid=(heads,),
            in_specs=[
                pl.BlockSpec((1, group, width), lambda i, meta: (jnp.minimum(i, count - 1), 0, 0)),
                pl.BlockSpec((1, group, width), lambda i, meta: (jnp.maximum(i - count, 0), 0, 0)),
                cached,
                cached,
            ],
            out_specs=[placed] * 3,
        ),
        compiler_params=pltpu.CompilerParams(vmem_limit_bytes=56 * 1024 * 1024),
        cost_estimate=pl.CostEstimate(
            flops=8 * group * (cache_len + group) * HEAD * heads,
            bytes_accessed=4 * (cache_len + 2 * group) * heads * HEAD,
            transcendentals=group * (cache_len + group) * heads,
        ),
    )(meta, own, other, cache_k, cache_v)


def output_kernel(meta_ref, *refs, blocks, groups, first):
    a_refs = [refs[g * blocks : (g + 1) * blocks] for g in range(groups)]
    w_ref = refs[groups * blocks]
    out_refs, (buf, sem) = refs[groups * blocks + 1 : -2], refs[-2:]
    _, chunk, head_cols = buf.shape
    half = head_cols // 2
    cols = half // groups
    ranked = output_order(blocks)
    for at, e in enumerate(ranked):
        for i in range(blocks):

            @pl.when(meta_ref[e] == i)
            def _(at=at, i=i):
                for g in range(groups):
                    for side in range(2):
                        pltpu.make_async_copy(
                            a_refs[g][i].at[pl.ds(first, chunk), pl.ds(side * cols, cols)],
                            buf.at[at, :, pl.ds(side * half + g * cols, cols)],
                            sem.at[at],
                        ).start()

    side = blocks // 2
    for part in range(2):
        for at in range(part * side, (part + 1) * side):
            pltpu.make_async_copy(buf.at[at], buf.at[at], sem.at[at]).wait()
        tokens = buf[part * side : (part + 1) * side].reshape(side * chunk, head_cols)
        product = jnp.dot(tokens, w_ref[...], preferred_element_type=F32).astype(BF16)
        out_refs[part][...] = product.reshape(out_refs[part].shape)


def output_order(blocks):
    bits = blocks.bit_length() - 1
    return sorted(range(blocks), key=lambda e: [1 - (e & 1)] + [e >> bit & 1 for bit in range(1, bits)])


def output(meta, gathered, w_out, first, chunk):
    groups, blocks = len(gathered), len(gathered[0])
    head_cols, out_cols = w_out.shape
    hbm = pl.BlockSpec(memory_space=pltpu.HBM)
    vmem = pl.BlockSpec(memory_space=pltpu.VMEM)
    return pl.pallas_call(
        functools.partial(output_kernel, blocks=blocks, groups=groups, first=first),
        out_shape=[jax.ShapeDtypeStruct((blocks // 2, chunk, out_cols), BF16)] * 2,
        in_specs=[pl.BlockSpec(memory_space=pltpu.SMEM)] + [hbm] * (groups * blocks) + [vmem],
        out_specs=[vmem] * 2,
        scratch_shapes=[pltpu.VMEM((blocks, chunk, head_cols), BF16), pltpu.SemaphoreType.DMA((blocks,))],
        compiler_params=pltpu.CompilerParams(vmem_limit_bytes=40 * 1024 * 1024),
        cost_estimate=pl.CostEstimate(
            flops=2 * blocks * chunk * head_cols * out_cols,
            bytes_accessed=2 * (blocks * chunk * (head_cols + out_cols) + head_cols * out_cols),
            transcendentals=0,
        ),
    )(meta, *[a for part in gathered for a in part], w_out)


def local(
    rows_n,
    cols_n,
    hidden_in,
    norm_gain,
    norm_bias,
    w_query,
    w_keyval,
    bias_query,
    bias_keyval,
    cache_keys,
    cache_values,
    cache_lengths,
    owner_slot,
    w_out,
    bias_out,
):
    row = lax.axis_index("row")
    col = lax.axis_index("col")
    core = row & 1
    group_len, width = hidden_in.shape
    slice_len, head_cols = w_query.shape
    half = head_cols // HEAD // 2
    half_cols = head_cols // 2
    pairs = rows_n // 2
    row_bits = rows_n.bit_length() - 1
    col_bits = cols_n.bit_length() - 1
    q_scale = HEAD ** (-0.5)
    slot_ids = jnp.arange(rows_n, dtype=jnp.int32)
    is_owner = owner_slot[:, None] == slot_ids[None, :]
    inverse = jnp.sum(jnp.where(is_owner, slot_ids[:, None], 0), axis=0).astype(jnp.int32)

    pair = row // 2
    pieces, core_after = normalize(jnp.stack([pair, core]).astype(jnp.int32), hidden_in, norm_gain, norm_bias, pairs)
    x_blocks = [None] * rows_n
    for offset in reversed(range(pairs)):
        piece = swap(pieces[offset], "row", 2 * offset, rows_n) if offset else pieces[0]
        x_blocks[2 * offset] = piece
        x_blocks[2 * offset + 1] = swap(piece, "row", 1, rows_n)

    def half_of(weight, which):
        part = lax.dynamic_slice_in_dim(weight, which * half_cols, half_cols, weight.ndim - 1)
        return part.reshape(slice_len, -1)

    w_kept = half_of(w_keyval, core_after)
    given = jnp.concatenate([half_of(w_query, 1 - core_after), half_of(w_keyval, 1 - core_after)], axis=1)
    taken = swap(given, "row", 1, rows_n)

    bias = jnp.concatenate([bias_query[None], bias_keyval], axis=0).reshape(3, 2, half, HEAD).transpose(1, 2, 0, 3)
    bias = lax.dynamic_index_in_dim(bias, core, 0, keepdims=False).reshape(half, 3 * HEAD)
    scale = jnp.concatenate([jnp.full((HEAD,), q_scale, F32), jnp.ones((2 * HEAD,), F32)])

    groups = 3 if half % 3 == 0 else 1
    per_group = half // groups
    counts = [per_group // 2, per_group - per_group // 2] if per_group > 1 else [1]
    pair_bits = list(range(1, row_bits))
    orders = [pair_bits[at % len(pair_bits) :] + pair_bits[: at % len(pair_bits)] for at in range(len(counts))]
    project_meta = jnp.concatenate([core[None], inverse[row ^ slot_ids] ^ row]).astype(jnp.int32)
    attend_meta = jnp.stack([cache_lengths[inverse[row]], core]).astype(jnp.int32)

    projected = [
        project(project_meta, x_blocks, w_query, w_kept, taken, g, per_group, orders, counts) for g in range(groups)
    ]
    key_parts, value_parts, gathered, finished = [], [], [], []
    for g in range(groups):
        base = g * per_group
        terms = [[projected[g][2 * p]] for p in range(len(orders))]
        sends = [projected[g][2 * p + 1] for p in range(len(orders))]
        for at in range(len(pair_bits)):
            for p, order in enumerate(orders):
                terms[p].append(swap(sends[p], "row", 1 << order[at], rows_n))
            if at + 1 < len(pair_bits):
                sends = forward(terms, finished[: g - 1] if g > 1 else [])
        mine, theirs = settle(terms, bias[base : base + per_group], scale[None], finished[-1:])
        came = swap(theirs, "row", 1, rows_n)
        attended, new_k, new_v = attend(attend_meta, mine, came, cache_keys, cache_values, base, half)
        finished.append(attended)
        key_parts.append(new_k)
        value_parts.append(new_v)
        every = [None] * rows_n
        for offset in reversed(range(pairs)):
            piece = swap(attended, "row", 2 * offset, rows_n) if offset else attended
            every[2 * offset] = piece
            every[2 * offset + 1] = swap(piece, "row", 1, rows_n)
        gathered.append(every)

    cols = per_group * HEAD
    new_k, new_v = (
        jnp.concatenate([p[:, side * cols : (side + 1) * cols] for side in range(2) for p in parts], axis=1)[None]
        for parts in (key_parts, value_parts)
    )

    places = (owner_slot[row ^ slot_ids] ^ row).astype(jnp.int32)
    shift = row_bits - col_bits
    low_bits = row & ((1 << shift) - 1)
    out_cols = width // cols_n
    residual = lax.dynamic_slice_in_dim(hidden_in, col * out_cols, out_cols, 1).astype(F32) + bias_out
    chunks = 4
    chunk = group_len // chunks
    results = []
    for c in range(chunks):
        send, keep = output(places, gathered, w_out, c * chunk, chunk)
        held = jnp.stack([keep, swap(send, "row", 1, rows_n)])
        for bit in range(1, row_bits):
            count = held.shape[1] // 2
            keep, came = held[:, :count], swap(held[:, count:], "row", 1 << bit, rows_n)
            if bit >= shift:
                flip = ((row >> bit) ^ (col >> (bit - shift))) & 1
                came, keep = (
                    swap(jnp.where(flip == 0, came, keep), "col", 1 << (bit - shift), cols_n),
                    jnp.where(flip == 0, keep, came),
                )
                held = keep.astype(F32) + came.astype(F32)
                held = held if bit == row_bits - 1 else held.astype(BF16)
            else:
                held = jnp.concatenate([keep, came], axis=0)
        count = 1 << shift
        results.append(
            jnp.concatenate(
                [lax.dynamic_index_in_dim(held[:, 0], low_bits ^ j, 0, keepdims=False) for j in range(count)], axis=1
            )
        )
    hidden_out = (jnp.concatenate(results, axis=0) + residual).astype(BF16)
    return hidden_out, new_k, new_v


def solution(mesh):
    placed = (
        P("row", None),
        P(),
        P(),
        P("row", "col"),
        P("row", None, "col"),
        P("col"),
        P(None, "col"),
        P("row", None, "col"),
        P("row", None, "col"),
        P(),
        P(),
        P("col", "row"),
        P("col"),
    )
    return jax.shard_map(
        functools.partial(local, mesh.shape["row"], mesh.shape["col"]),
        mesh=mesh,
        in_specs=placed,
        out_specs=(P("row", "col"), P("row", None, "col"), P("row", None, "col")),
        check_vma=False,
    )
```

```python
import functools

import jax
import jax.numpy as jnp
from jax import lax
from jax.experimental import pallas as pl
from jax.experimental.pallas import tpu as pltpu
from jax.sharding import PartitionSpec as P

HEAD = 128
F32 = jnp.float32
MIB = 1024 * 1024
SMALL = pl.CostEstimate(flops=1, bytes_accessed=1, transcendentals=0)
BF16 = jnp.bfloat16


def normalize_kernel(meta_ref, hidden_ref, gain_ref, bias_ref, *out_refs):
    piece_refs = out_refs
    width = hidden_ref.shape[1]
    length = piece_refs[0].shape[1]
    rows = hidden_ref[...].astype(F32)
    mean = jnp.sum(rows, axis=1, keepdims=True) / width
    centered = rows - mean
    var = jnp.sum(centered * centered, axis=1, keepdims=True) / width
    factor = lax.rsqrt(var + 1e-05)
    for d, ref in enumerate(piece_refs):
        part = pl.ds(pl.multiple_of((meta_ref[0] ^ d) * length, HEAD), length)
        ref[...] = ((hidden_ref[:, part].astype(F32) - mean) * factor * gain_ref[:, part] + bias_ref[:, part]).astype(BF16)


def normalize(meta, hidden, gain, bias, pairs):
    rows, width = hidden.shape
    step = 32
    whole = pl.BlockSpec((1, width), lambda i, meta: (0, 0))
    return pl.pallas_call(
        normalize_kernel,
        out_shape=[jax.ShapeDtypeStruct((rows, width // pairs), BF16)] * pairs,
        grid_spec=pltpu.PrefetchScalarGridSpec(
            num_scalar_prefetch=1,
            grid=(rows // step,),
            in_specs=[pl.BlockSpec((step, width), lambda i, meta: (i, 0)), whole, whole],
            out_specs=[pl.BlockSpec((step, width // pairs), lambda i, meta: (i, 0))] * pairs,
        ),
        compiler_params=pltpu.CompilerParams(vmem_limit_bytes=60 * MIB),
        cost_estimate=SMALL,
    )(meta, hidden, gain[None], bias[None])


def weave_kernel(meta_ref, q_ref, kv_ref, taken_q_ref, taken_kv_ref, *refs, cuts, behind):
    (out_ref,) = refs[behind:]

    def weave(queries_ref, keyval_ref):
        at = 0
        for first, last in cuts:
            for kind in range(3):
                cols = pl.ds(first * HEAD, (last - first) * HEAD)
                part = queries_ref[:, cols] if kind == 0 else keyval_ref[:, kind - 1, cols]
                out_ref[:, pl.ds(at, (last - first) * HEAD)] = part
                at += (last - first) * HEAD

    @pl.when(pl.program_id(0) == 0)
    def _():
        weave(q_ref, kv_ref)

    @pl.when(pl.program_id(0) != 0)
    def _():
        weave(taken_q_ref, taken_kv_ref)


def weave(core, w_query, w_keyval, taken_query, taken_keyval, cuts, behind):
    rows, cols = w_query.shape
    half = cols // 2
    step = 128 if rows % 128 == 0 else 64
    steps = rows // step
    own = lambda side, i, meta: jnp.where(side == 0, i, steps - 1)
    other = lambda side, i, meta: jnp.where(side == 0, 0, i)
    specs = []
    for place in (own, other):
        specs.append(pl.BlockSpec((step, half), lambda side, i, meta, place=place: (place(side, i, meta), meta[0])))
        specs.append(pl.BlockSpec((step, 2, half), lambda side, i, meta, place=place: (place(side, i, meta), 0, meta[0])))
    return pl.pallas_call(
        functools.partial(weave_kernel, cuts=cuts, behind=len(behind)),
        out_shape=jax.ShapeDtypeStruct((2 * rows, 3 * half), BF16),
        grid_spec=pltpu.PrefetchScalarGridSpec(
            num_scalar_prefetch=1,
            grid=(2, steps),
            in_specs=specs + [pl.BlockSpec(memory_space=pl.ANY)] * len(behind),
            out_specs=pl.BlockSpec((step, 3 * half), lambda side, i, meta: ((meta[0] ^ side) * steps + i, 0)),
        ),
        compiler_params=pltpu.CompilerParams(vmem_limit_bytes=40 * MIB),
        cost_estimate=SMALL,
    )(core.reshape(1).astype(jnp.int32), w_query, w_keyval, taken_query, taken_keyval, *behind)


def fetch_kernel(*refs, count, behind):
    out_refs, sem = refs[count + behind : -1], refs[-1]
    copies = [pltpu.make_async_copy(refs[at], out_refs[at], sem.at[at]) for at in range(count)]
    for copy in copies:
        copy.start()
    for copy in copies:
        copy.wait()


def fetch(sources, behind):
    space = pl.BlockSpec(memory_space=pl.ANY)
    return pl.pallas_call(
        functools.partial(fetch_kernel, count=len(sources), behind=len(behind)),
        out_shape=[jax.ShapeDtypeStruct(source.shape, source.dtype) for source in sources],
        in_specs=[space] * (len(sources) + len(behind)),
        out_specs=[pl.BlockSpec(memory_space=pltpu.VMEM)] * len(sources),
        scratch_shapes=[pltpu.SemaphoreType.DMA((len(sources),))],
        cost_estimate=SMALL,
    )(*sources, *behind)


def swap(value, axis, mask, size):
    return lax.ppermute(value, axis, [(i, i ^ mask) for i in range(size)])


def gather_block(table, places, dst, sem):
    for at, place in enumerate(places):

        @pl.when(table == at)
        def _(place=place):
            pltpu.make_async_copy(place, dst, sem).start()


def project_kernel(meta_ref, *refs, blocks, group, orders, behind):
    x_refs, w_ref = refs[:blocks], refs[blocks]
    out_refs, (x_buf, w_buf, x_sem, w_sem) = refs[blocks + 1 + behind : -4], refs[-4:]
    cols = w_buf.shape[1] // 3
    load = pltpu.make_async_copy(w_ref.at[:, pl.ds(group * 3 * cols, 3 * cols)], w_buf, w_sem)
    load.start()
    sequence = sorted(range(blocks), key=lambda e: -sum(bool(e >> order[0] & 1) for order in orders))
    for at, e in enumerate(sequence):
        gather_block(meta_ref[e], x_refs, x_buf.at[at], x_sem.at[at])
    load.wait()
    group_len = x_buf.shape[1]
    batch = 2
    for start in range(0, blocks, batch):
        for at in range(start, start + batch):
            pltpu.make_async_copy(x_refs[0], x_buf.at[at], x_sem.at[at]).wait()
        tokens = x_buf[start : start + batch].reshape(batch * group_len, x_buf.shape[2])
        product = jnp.dot(tokens, w_buf[...], preferred_element_type=F32).astype(BF16)
        first = 0
        for p, order in enumerate(orders):
            keep_ref, send_ref = out_refs[2 * p], out_refs[2 * p + 1]
            count = keep_ref.shape[2] // (3 * HEAD)
            ranked = slots_in(blocks, order)
            for c in range(batch):
                place = ranked.index(sequence[start + c])
                ref = keep_ref if place < blocks // 2 else send_ref
                for h in range(count):
                    for kind in range(3):
                        at = kind * cols + (first + h) * HEAD
                        ref[place % (blocks // 2), :, pl.ds((3 * h + kind) * HEAD, HEAD)] = product[
                            c * group_len : (c + 1) * group_len, at : at + HEAD
                        ]
            first += count


def slots_in(blocks, order):
    return sorted(range(blocks), key=lambda e: [e >> bit & 1 for bit in order] + [e & 1])


def project(meta, x_blocks, weights, group, per_group, orders, counts, behind):
    blocks = len(x_blocks)
    group_len, depth = x_blocks[0].shape
    any_space = pl.BlockSpec(memory_space=pl.ANY)
    out_shape = []
    for count in counts:
        out_shape += [jax.ShapeDtypeStruct((blocks // 2, group_len, count * 3 * HEAD), BF16)] * 2
    cols = per_group * 3 * HEAD
    return pl.pallas_call(
        functools.partial(project_kernel, blocks=blocks, group=group, orders=orders, behind=len(behind)),
        out_shape=out_shape,
        in_specs=[pl.BlockSpec(memory_space=pltpu.SMEM)] + [any_space] * (blocks + 1 + len(behind)),
        out_specs=[pl.BlockSpec(memory_space=pltpu.VMEM)] * len(out_shape),
        scratch_shapes=[
            pltpu.VMEM((blocks, group_len, depth), BF16),
            pltpu.VMEM((depth, cols), BF16),
            pltpu.SemaphoreType.DMA((blocks,)),
            pltpu.SemaphoreType.DMA(()),
        ],
        compiler_params=pltpu.CompilerParams(vmem_limit_bytes=60 * MIB),
        cost_estimate=SMALL,
    )(meta, *x_blocks, weights, *behind)


def forward_kernel(*refs, parts, terms, behind):
    out_refs = refs[parts * terms + behind :]
    for p in range(parts):
        mine = refs[p * terms : (p + 1) * terms]
        out_refs[p][...] = sum(ref[...].astype(F32) for ref in mine).astype(BF16)


def forward(terms, behind):
    left = min(t.shape[0] for t in terms[0]) // 2
    shapes = [(left, *ts[0].shape[1:]) for ts in terms]
    specs = [pl.BlockSpec(shape, lambda i: (1, 0, 0)) for shape, ts in zip(shapes, terms) for _ in ts]
    return pl.pallas_call(
        functools.partial(forward_kernel, parts=len(terms), terms=len(terms[0]), behind=len(behind)),
        grid=(1,),
        out_shape=[jax.ShapeDtypeStruct(shape, BF16) for shape in shapes],
        in_specs=specs + [pl.BlockSpec(memory_space=pl.ANY)] * len(behind),
        out_specs=[pl.BlockSpec(shape, lambda i: (0, 0, 0)) for shape in shapes],
        compiler_params=pltpu.CompilerParams(vmem_limit_bytes=24 * MIB),
        cost_estimate=SMALL,
    )(*[t for ts in terms for t in ts], *behind)


def settle_kernel(bias_ref, scale_ref, *refs, parts, terms, behind):
    mine_ref, theirs_ref = refs[parts * terms + behind :]
    width = mine_ref.shape[2]
    head = 0
    for p in range(parts):
        for h in range(refs[p * terms].shape[2] // width):
            cols = pl.ds(h * width, width)
            for e, ref in enumerate((mine_ref, theirs_ref)):
                total = sum(t[e, :, cols].astype(F32) for t in refs[p * terms : (p + 1) * terms])
                ref[head] = ((total + bias_ref[head : head + 1, :]) * scale_ref[...]).astype(BF16)
            head += 1


def settle(terms, bias, scale, behind):
    heads, width = bias.shape
    rows = terms[0][0].shape[1]
    specs = [pl.BlockSpec((2, *t.shape[1:]), lambda i: (0, 0, 0)) for ts in terms for t in ts]
    whole = pl.BlockSpec((heads, rows, width), lambda i: (0, 0, 0))
    return pl.pallas_call(
        functools.partial(settle_kernel, parts=len(terms), terms=len(terms[0]), behind=len(behind)),
        grid=(1,),
        out_shape=[jax.ShapeDtypeStruct((heads, rows, width), BF16)] * 2,
        in_specs=[pl.BlockSpec((heads, width), lambda i: (0, 0)), pl.BlockSpec((1, width), lambda i: (0, 0))]
        + specs
        + [pl.BlockSpec(memory_space=pl.ANY)] * len(behind),
        out_specs=[whole, whole],
        compiler_params=pltpu.CompilerParams(vmem_limit_bytes=24 * MIB),
        cost_estimate=SMALL,
    )(bias, scale, *[t for ts in terms for t in ts], *behind)


def attend_kernel(meta_ref, own_ref, other_ref, k_ref, v_ref, *refs, key_len, behind):
    o_ref, nk_ref, nv_ref = refs[behind:]
    length = meta_ref[0]
    qkv = jnp.where(pl.program_id(0) < pl.num_programs(0) // 2, own_ref[0], other_ref[0])
    q, new_k, new_v = qkv[:, :HEAD], qkv[:, HEAD : 2 * HEAD], qkv[:, 2 * HEAD :]
    nk_ref[...] = new_k
    nv_ref[...] = new_v
    group = q.shape[0]
    cache_len = k_ref.shape[1]

    def scores_of(at):
        keys = k_ref[0, at : at + key_len, :]
        scores = lax.dot_general(q, keys, (((1,), (1,)), ((), ())), preferred_element_type=F32)
        positions = at + lax.broadcasted_iota(jnp.int32, (1, key_len), 1)
        return jnp.where(positions < length, scores, -1e30)

    def lane_sum(probs):
        total = probs[:, :HEAD]
        for at in range(HEAD, probs.shape[1], HEAD):
            total = total + probs[:, at : at + HEAD]
        return total

    rows = lax.broadcasted_iota(jnp.int32, (group, group), 0)
    cols = lax.broadcasted_iota(jnp.int32, (group, group), 1)
    scores = lax.dot_general(q, new_k, (((1,), (1,)), ((), ())), preferred_element_type=F32)
    scores = jnp.where(cols <= rows, scores, -1e30)
    following = scores_of(0)
    row_max = jnp.max(scores, axis=1, keepdims=True)
    probs = jnp.exp(scores - row_max)
    row_sum = lane_sum(probs)
    weighted = jnp.dot(probs.astype(BF16), new_v, preferred_element_type=F32)
    for at in range(0, cache_len, key_len):
        scores = following
        if at + key_len < cache_len:
            following = scores_of(at + key_len)
        new_max = jnp.maximum(row_max, jnp.max(scores, axis=1, keepdims=True))
        factor = jnp.exp(row_max - new_max)
        probs = jnp.exp(scores - new_max)
        row_max = new_max
        row_sum = row_sum * factor + lane_sum(probs)
        values = v_ref[0, at : at + key_len, :]
        weighted = weighted * factor + jnp.dot(probs.astype(BF16), values, preferred_element_type=F32)
    total = jnp.sum(row_sum, axis=1, keepdims=True)
    o_ref[...] = (weighted / total).astype(BF16)


def attend(meta, own, other, cache_k, cache_v, base, half, behind):
    count, group, width = own.shape
    heads = 2 * count
    cache_len = cache_k.shape[1]
    key_len = min(512, cache_len)

    def side(i, meta):
        return (i // count) ^ meta[1]

    cached = pl.BlockSpec((1, cache_len, HEAD), lambda i, meta: (0, 0, side(i, meta) * half + base + i % count))
    placed = pl.BlockSpec((group, HEAD), lambda i, meta: (0, side(i, meta) * count + i % count))
    return pl.pallas_call(
        functools.partial(attend_kernel, key_len=key_len, behind=len(behind)),
        out_shape=[jax.ShapeDtypeStruct((group, heads * HEAD), BF16)] * 3,
        grid_spec=pltpu.PrefetchScalarGridSpec(
            num_scalar_prefetch=1,
            grid=(heads,),
            in_specs=[
                pl.BlockSpec((1, group, width), lambda i, meta: (jnp.minimum(i, count - 1), 0, 0)),
                pl.BlockSpec((1, group, width), lambda i, meta: (jnp.maximum(i - count, 0), 0, 0)),
                cached,
                cached,
            ]
            + [pl.BlockSpec(memory_space=pl.ANY)] * len(behind),
            out_specs=[placed] * 3,
        ),
        compiler_params=pltpu.CompilerParams(vmem_limit_bytes=60 * MIB),
        cost_estimate=SMALL,
    )(meta, own, other, cache_k, cache_v, *behind)


def output_kernel(*refs, pairs, groups):
    a_refs = [refs[g * pairs : (g + 1) * pairs] for g in range(groups)]
    w_refs = refs[groups * pairs : groups * pairs + 2]
    out_refs, (buf, sem) = refs[groups * pairs + 2 : -2], refs[-2:]
    _, rows, head_cols = buf.shape
    half = head_cols // 2
    cols = half // groups
    chunk = rows // len(out_refs)
    for d in range(pairs):
        for g in range(groups):
            for side in range(2):
                pltpu.make_async_copy(
                    a_refs[g][d].at[:, pl.ds(side * cols, cols)],
                    buf.at[d, :, pl.ds(side * half + g * cols, cols)],
                    sem.at[d],
                ).start()
    for d in range(pairs):
        pltpu.make_async_copy(buf.at[d], buf.at[d], sem.at[d]).wait()
    for d in range(0, pairs, 2):
        tokens = buf[d : d + 2].reshape(2 * rows, head_cols)
        for j in range(2):
            product = jnp.dot(tokens, w_refs[j][...], preferred_element_type=F32).astype(BF16)
            for c, out_ref in enumerate(out_refs):
                for at in range(2):
                    first = at * rows + c * chunk
                    out_ref[j, d + at] = product[first : first + chunk]


def output(gathered, w_pair, chunks):
    groups, pairs = len(gathered), len(gathered[0])
    rows = gathered[0][0].shape[0]
    head_cols, out_cols = w_pair[0].shape
    space = pl.BlockSpec(memory_space=pl.ANY)
    vmem = pl.BlockSpec(memory_space=pltpu.VMEM)
    return pl.pallas_call(
        functools.partial(output_kernel, pairs=pairs, groups=groups),
        out_shape=[jax.ShapeDtypeStruct((2, pairs, rows // chunks, out_cols), BF16)] * chunks,
        in_specs=[space] * (groups * pairs) + [vmem] * 2,
        out_specs=[vmem] * chunks,
        scratch_shapes=[pltpu.VMEM((pairs, rows, head_cols), BF16), pltpu.SemaphoreType.DMA((pairs,))],
        compiler_params=pltpu.CompilerParams(vmem_limit_bytes=40 * MIB),
        cost_estimate=SMALL,
    )(*[a for part in gathered for a in part], *w_pair)


def block_call(kernel, out_shapes, scalars, arrays, shapes, indices, behind):
    return pl.pallas_call(
        functools.partial(kernel, behind=len(behind)),
        out_shape=[jax.ShapeDtypeStruct(shape, BF16) for shape in out_shapes],
        grid_spec=pltpu.PrefetchScalarGridSpec(
            num_scalar_prefetch=1,
            grid=(1,),
            in_specs=[pl.BlockSpec(shape, index) for shape, index in zip(shapes, indices)]
            + [pl.BlockSpec(memory_space=pl.ANY)] * len(behind),
            out_specs=[
                pl.BlockSpec(shape, lambda i, meta, rank=len(shape): (0,) * rank) for shape in out_shapes
            ],
        ),
        compiler_params=pltpu.CompilerParams(vmem_limit_bytes=16 * MIB),
        cost_estimate=SMALL,
    )(scalars, *arrays, *behind)


def split_pair_kernel(meta_ref, own_ref, came_ref, *refs, behind):
    mine_ref, sent_ref = refs[behind:]
    count = mine_ref.shape[1]
    pairs = 2 * count
    offsets = slots_in(2 * pairs, range(1, pairs.bit_length()))[::2]
    for at, e in enumerate(offsets):
        place = meta_ref[e]
        for j in range(2):
            block = jnp.where(place % 2 == 0, own_ref[j, place // 2], came_ref[1 - j, place // 2])
            if at < count:
                mine_ref[j, at] = block
            else:
                sent_ref[j, at - count] = block


def split_pair(places, own, came, behind):
    _, pairs, chunk, cols = own.shape
    first = lambda i, meta: (0, 0, 0, 0)
    shapes = [(2, pairs // 2, chunk, cols)] * 2
    return block_call(split_pair_kernel, shapes, places, [own, came], [own.shape] * 2, [first] * 2, behind)


def choose_kernel(meta_ref, keep_ref, came_ref, *refs, behind):
    mine_ref, sent_ref = refs[behind:]

    @pl.when(meta_ref[0] == 0)
    def _():
        mine_ref[...] = keep_ref[...]
        sent_ref[...] = came_ref[...]

    @pl.when(meta_ref[0] != 0)
    def _():
        mine_ref[...] = came_ref[...]
        sent_ref[...] = keep_ref[...]


def choose(flip, keep, came, behind):
    first = lambda i, meta: (0,) * keep.ndim
    return block_call(choose_kernel, [keep.shape] * 2, flip, [keep, came], [keep.shape] * 2, [first] * 2, behind)


def add_split_kernel(meta_ref, keep_ref, came_ref, *refs, behind):
    mine_ref, sent_ref = refs[behind:]
    count = mine_ref.shape[1]
    total = (keep_ref[...].astype(F32) + came_ref[...].astype(F32)).astype(BF16)
    mine_ref[...] = total[:, :count]
    sent_ref[...] = total[:, count:]


def add_split(keep, came, behind):
    slices, count, chunk, cols = keep.shape
    first = lambda i, meta: (0, 0, 0, 0)
    shapes = [(slices, count // 2, chunk, cols)] * 2
    scalars = jnp.zeros((1,), jnp.int32)
    return block_call(add_split_kernel, shapes, scalars, [keep, came], [keep.shape] * 2, [first] * 2, behind)


def finish_rows_kernel(meta_ref, keep_ref, came_ref, hidden_ref, bias_ref, *refs, behind):
    (out_ref,) = refs[behind:]
    cols = keep_ref.shape[3]
    total = [keep_ref[j, 0].astype(F32) + came_ref[j, 0].astype(F32) for j in range(2)]
    for side in range(2):
        at = pl.ds(side * cols, cols)
        part = jnp.where(meta_ref[0] == side, total[0], total[1])
        out_ref[:, at] = (part + bias_ref[:, at] + hidden_ref[:, at].astype(F32)).astype(BF16)


def finish_rows(meta, keep, came, hidden, bias, at, behind):
    chunk, cols = keep.shape[2:]
    width = 2 * cols
    shapes = [keep.shape, keep.shape, (chunk, width), (1, width)]
    first = lambda i, meta: (0, 0, 0, 0)
    indices = [first, first, lambda i, meta: (at, meta[1]), lambda i, meta: (0, 0)]
    arrays = [keep, came, hidden, bias[None]]
    return block_call(finish_rows_kernel, [(chunk, width)], meta, arrays, shapes, indices, behind)[0]


def local(
    rows_n,
    cols_n,
    hidden_in,
    norm_gain,
    norm_bias,
    w_query,
    w_keyval,
    bias_query,
    bias_keyval,
    cache_keys,
    cache_values,
    cache_lengths,
    owner_slot,
    w_out,
    bias_out,
):
    row = lax.axis_index("row")
    col = lax.axis_index("col")
    core = row & 1
    group_len, width = hidden_in.shape
    slice_len, head_cols = w_query.shape
    half = head_cols // HEAD // 2
    half_cols = head_cols // 2
    pairs = rows_n // 2
    row_bits = rows_n.bit_length() - 1
    col_bits = cols_n.bit_length() - 1
    q_scale = HEAD ** (-0.5)
    slot_ids = jnp.arange(rows_n, dtype=jnp.int32)
    is_owner = owner_slot[:, None] == slot_ids[None, :]
    inverse = jnp.sum(jnp.where(is_owner, slot_ids[:, None], 0), axis=0).astype(jnp.int32)

    pair = row // 2
    pieces = normalize(pair.reshape(1).astype(jnp.int32), hidden_in, norm_gain, norm_bias, pairs)
    x_blocks = [None] * rows_n
    for offset in reversed(range(pairs)):
        piece = swap(pieces[offset], "row", 2 * offset, rows_n) if offset else pieces[0]
        x_blocks[2 * offset] = piece

    groups = 3 if half % 3 == 0 else 1
    per_group = half // groups
    parts = [(g * per_group, (g + 1) * per_group) for g in range(groups)]
    taken = swap(w_query, "row", 1, rows_n), swap(w_keyval, "row", 1, rows_n)
    weights = weave(core, w_query, w_keyval, *taken, parts, [pieces[0]])
    w_pair = w_out, swap(w_out, "row", 1, rows_n)
    arrived = fetch(x_blocks[2::2], [weights, w_pair[1]])
    for offset in range(pairs):
        x_blocks[2 * offset + 1] = swap(arrived[offset - 1] if offset else x_blocks[0], "row", 1, rows_n)

    bias = jnp.concatenate([bias_query[None], bias_keyval], axis=0).reshape(3, 2, half, HEAD).transpose(1, 2, 0, 3)
    bias = lax.dynamic_index_in_dim(bias, core, 0, keepdims=False).reshape(half, 3 * HEAD)
    scale = jnp.concatenate([jnp.full((HEAD,), q_scale, F32), jnp.ones((2 * HEAD,), F32)])

    counts = [per_group // 2, per_group - per_group // 2] if per_group > 1 else [1]
    pair_bits = list(range(1, row_bits))
    orders = [pair_bits[at % len(pair_bits) :] + pair_bits[: at % len(pair_bits)] for at in range(len(counts))]
    project_meta = (inverse[row ^ slot_ids] ^ row).astype(jnp.int32)
    attend_meta = jnp.stack([cache_lengths[inverse[row]], core]).astype(jnp.int32)

    def project_group(g, behind):
        return project(project_meta, x_blocks, weights, g, per_group, orders, counts, behind)

    projected = [project_group(0, [])]
    key_parts, value_parts, gathered, finished, waiting = [], [], [], [], []

    def finish(g):
        base = g * per_group
        mine, theirs = settle(
            waiting[g],
            bias[base : base + per_group],
            scale[None],
            finished[-1:] + ([projected[g + 2][0]] if g + 2 < groups else []),
        )
        came = swap(theirs, "row", 1, rows_n)
        attended, new_k, new_v = attend(
            attend_meta, mine, came, cache_keys, cache_values, base, half, gathered[0][1:] if g == 1 else []
        )
        finished.append(attended)
        key_parts.append(new_k)
        value_parts.append(new_v)
        gathered.append([swap(attended, "row", 2 * d, rows_n) if d else attended for d in range(pairs)])

    for g in range(groups):
        terms = [[projected[g][2 * p]] for p in range(len(orders))]
        sends = [projected[g][2 * p + 1] for p in range(len(orders))]
        if g + 1 < groups:
            projected.append(project_group(g + 1, [sent] if g else [projected[0][0]]))
        for at in range(len(pair_bits)):
            for p, order in enumerate(orders):
                terms[p].append(swap(sends[p], "row", 1 << order[at], rows_n))
            if at + 1 < len(pair_bits):
                sends = forward(terms, finished[-1:] + ([projected[g + 1][0]] if g + 1 < groups else []))
                sent = sends[0]
        waiting.append(terms)
        if g:
            finish(g - 1)
    finish(groups - 1)

    cols = per_group * HEAD
    new_k, new_v = (
        jnp.concatenate([p[:, side * cols : (side + 1) * cols] for side in range(2) for p in parts], axis=1)[None]
        for parts in (key_parts, value_parts)
    )

    places = (owner_slot[row ^ slot_ids] ^ row).astype(jnp.int32)
    shift = row_bits - col_bits
    if shift != 1:
        raise ValueError("unexpected mesh")
    chunks = 4
    chunk = group_len // chunks
    last = row_bits - 1
    flips = [((row >> bit) ^ (col >> (bit - 1))) & 1 for bit in range(1, row_bits)]
    flips = [flip.reshape(1).astype(jnp.int32) for flip in flips]
    final_meta = jnp.stack([core, col]).astype(jnp.int32)
    late = [0, 0] + [at for bit in range(1, last) for at in (4.5 * bit + 1.5, 4.5 * bit + 4.5)]
    late += [4.5 * last + 1.5, 4.5 * last + 4.6]
    order = sorted((c * (2 if step > 1 else 0.5) + late[step], step, c) for c in range(chunks) for step in range(1, 2 * last + 2))
    products = output(gathered, w_pair, chunks)
    state = {c: (product, swap(product, "row", 1, rows_n)) for c, product in enumerate(products)}
    done, order_behind = {}, []
    for _, step, c in order:
        if step == 2 * last + 1:
            done[c] = finish_rows(final_meta, *state[c], hidden_in, bias_out, c, order_behind)
            order_behind = [done[c]]
        else:
            bit = (step + 1) // 2
            if step == 1:
                keep, sent = split_pair(places, *state[c], order_behind)
            elif step % 2:
                keep, sent = add_split(*state[c], order_behind)
            else:
                keep, sent = choose(flips[bit - 1], *state[c], order_behind)
            axis, mask, size = ("row", 1 << bit, rows_n) if step % 2 else ("col", 1 << (bit - 1), cols_n)
            state[c] = (keep, swap(sent, axis, mask, size))
            order_behind = [sent]
    hidden_out = jnp.concatenate([done[c] for c in range(chunks)], axis=0)
    return hidden_out, new_k, new_v


def solution(mesh):
    placed = (
        P("row", None),
        P(),
        P(),
        P("row", "col"),
        P("row", None, "col"),
        P("col"),
        P(None, "col"),
        P("row", None, "col"),
        P("row", None, "col"),
        P(),
        P(),
        P("col", "row"),
        P("col"),
    )
    return jax.shard_map(
        functools.partial(local, mesh.shape["row"], mesh.shape["col"]),
        mesh=mesh,
        in_specs=placed,
        out_specs=(P("row", "col"), P("row", None, "col"), P("row", None, "col")),
        check_vma=False,
    )
```

```python
import functools

import jax
import jax.numpy as jnp
from jax import lax
from jax.experimental import pallas as pl
from jax.experimental.pallas import tpu as pltpu
from jax.sharding import PartitionSpec as P

HEAD = 128
F32 = jnp.float32
MIB = 1024 * 1024
SMALL = pl.CostEstimate(flops=1, bytes_accessed=1, transcendentals=0)
BF16 = jnp.bfloat16


def normalize_kernel(meta_ref, hidden_ref, gain_ref, bias_ref, *out_refs):
    piece_refs = out_refs
    width = hidden_ref.shape[1]
    length = piece_refs[0].shape[1]
    rows = hidden_ref[...].astype(F32)
    mean = jnp.sum(rows, axis=1, keepdims=True) / width
    centered = rows - mean
    var = jnp.sum(centered * centered, axis=1, keepdims=True) / width
    factor = lax.rsqrt(var + 1e-05)
    for d, ref in enumerate(piece_refs):
        part = pl.ds(pl.multiple_of((meta_ref[0] ^ d) * length, HEAD), length)
        ref[...] = ((hidden_ref[:, part].astype(F32) - mean) * factor * gain_ref[:, part] + bias_ref[:, part]).astype(BF16)


def normalize(meta, hidden, gain, bias, pairs):
    rows, width = hidden.shape
    step = 32
    whole = pl.BlockSpec((1, width), lambda i, meta: (0, 0))
    return pl.pallas_call(
        normalize_kernel,
        out_shape=[jax.ShapeDtypeStruct((rows, width // pairs), BF16)] * pairs,
        grid_spec=pltpu.PrefetchScalarGridSpec(
            num_scalar_prefetch=1,
            grid=(rows // step,),
            in_specs=[pl.BlockSpec((step, width), lambda i, meta: (i, 0)), whole, whole],
            out_specs=[pl.BlockSpec((step, width // pairs), lambda i, meta: (i, 0))] * pairs,
        ),
        compiler_params=pltpu.CompilerParams(vmem_limit_bytes=60 * MIB),
        cost_estimate=SMALL,
    )(meta, hidden, gain[None], bias[None])


def weave_kernel(meta_ref, q_ref, kv_ref, taken_q_ref, taken_kv_ref, *refs, cuts, behind):
    (out_ref,) = refs[behind:]

    def weave(queries_ref, keyval_ref):
        at = 0
        for first, last in cuts:
            for kind in range(3):
                cols = pl.ds(first * HEAD, (last - first) * HEAD)
                part = queries_ref[:, cols] if kind == 0 else keyval_ref[:, kind - 1, cols]
                out_ref[:, pl.ds(at, (last - first) * HEAD)] = part
                at += (last - first) * HEAD

    @pl.when(pl.program_id(0) == 0)
    def _():
        weave(q_ref, kv_ref)

    @pl.when(pl.program_id(0) != 0)
    def _():
        weave(taken_q_ref, taken_kv_ref)


def weave(core, w_query, w_keyval, taken_query, taken_keyval, cuts, behind):
    rows, cols = w_query.shape
    half = cols // 2
    step = 128 if rows % 128 == 0 else 64
    steps = rows // step
    own = lambda side, i, meta: jnp.where(side == 0, i, steps - 1)
    other = lambda side, i, meta: jnp.where(side == 0, 0, i)
    specs = []
    for place in (own, other):
        specs.append(pl.BlockSpec((step, half), lambda side, i, meta, place=place: (place(side, i, meta), meta[0])))
        specs.append(pl.BlockSpec((step, 2, half), lambda side, i, meta, place=place: (place(side, i, meta), 0, meta[0])))
    return pl.pallas_call(
        functools.partial(weave_kernel, cuts=cuts, behind=len(behind)),
        out_shape=jax.ShapeDtypeStruct((2 * rows, 3 * half), BF16),
        grid_spec=pltpu.PrefetchScalarGridSpec(
            num_scalar_prefetch=1,
            grid=(2, steps),
            in_specs=specs + [pl.BlockSpec(memory_space=pl.ANY)] * len(behind),
            out_specs=pl.BlockSpec((step, 3 * half), lambda side, i, meta: ((meta[0] ^ side) * steps + i, 0)),
        ),
        compiler_params=pltpu.CompilerParams(vmem_limit_bytes=60 * MIB),
        cost_estimate=SMALL,
    )(core.reshape(1).astype(jnp.int32), w_query, w_keyval, taken_query, taken_keyval, *behind)


def fetch_kernel(*refs, count, behind):
    out_refs, sem = refs[count + behind : -1], refs[-1]
    copies = [pltpu.make_async_copy(refs[at], out_refs[at], sem.at[at]) for at in range(count)]
    for copy in copies:
        copy.start()
    for copy in copies:
        copy.wait()


def fetch(sources, behind):
    space = pl.BlockSpec(memory_space=pl.ANY)
    return pl.pallas_call(
        functools.partial(fetch_kernel, count=len(sources), behind=len(behind)),
        out_shape=[jax.ShapeDtypeStruct(source.shape, source.dtype) for source in sources],
        in_specs=[space] * (len(sources) + len(behind)),
        out_specs=[pl.BlockSpec(memory_space=pltpu.VMEM)] * len(sources),
        scratch_shapes=[pltpu.SemaphoreType.DMA((len(sources),))],
        compiler_params=pltpu.CompilerParams(vmem_limit_bytes=60 * MIB),
        cost_estimate=SMALL,
    )(*sources, *behind)


def swap(value, axis, mask, size):
    return lax.ppermute(value, axis, [(i, i ^ mask) for i in range(size)])


def gather_block(table, places, dst, sem):
    for at, place in enumerate(places):

        @pl.when(table == at)
        def _(place=place):
            pltpu.make_async_copy(place, dst, sem).start()


def project_kernel(meta_ref, *refs, blocks, group, orders, behind):
    x_refs, w_ref = refs[:blocks], refs[blocks]
    out_refs, (x_buf, w_buf, x_sem, w_sem) = refs[blocks + 1 + behind : -4], refs[-4:]
    cols = w_buf.shape[1] // 3
    load = pltpu.make_async_copy(w_ref.at[:, pl.ds(group * 3 * cols, 3 * cols)], w_buf, w_sem)
    load.start()
    sequence = sorted(range(blocks), key=lambda e: -sum(bool(e >> order[0] & 1) for order in orders))
    for at, e in enumerate(sequence):
        gather_block(meta_ref[e], x_refs, x_buf.at[at], x_sem.at[at])
    load.wait()
    group_len = x_buf.shape[1]
    batch = 2
    for start in range(0, blocks, batch):
        for at in range(start, start + batch):
            pltpu.make_async_copy(x_refs[0], x_buf.at[at], x_sem.at[at]).wait()
        tokens = x_buf[start : start + batch].reshape(batch * group_len, x_buf.shape[2])
        product = jnp.dot(tokens, w_buf[...], preferred_element_type=F32).astype(BF16)
        first = 0
        for p, order in enumerate(orders):
            keep_ref, send_ref = out_refs[2 * p], out_refs[2 * p + 1]
            count = keep_ref.shape[2] // (3 * HEAD)
            ranked = slots_in(blocks, order)
            for c in range(batch):
                place = ranked.index(sequence[start + c])
                ref = keep_ref if place < blocks // 2 else send_ref
                for h in range(count):
                    for kind in range(3):
                        at = kind * cols + (first + h) * HEAD
                        ref[place % (blocks // 2), :, pl.ds((3 * h + kind) * HEAD, HEAD)] = product[
                            c * group_len : (c + 1) * group_len, at : at + HEAD
                        ]
            first += count


def slots_in(blocks, order):
    return sorted(range(blocks), key=lambda e: [e >> bit & 1 for bit in order] + [e & 1])


def project(meta, x_blocks, weights, group, per_group, orders, counts, behind):
    blocks = len(x_blocks)
    group_len, depth = x_blocks[0].shape
    any_space = pl.BlockSpec(memory_space=pl.ANY)
    out_shape = []
    for count in counts:
        out_shape += [jax.ShapeDtypeStruct((blocks // 2, group_len, count * 3 * HEAD), BF16)] * 2
    cols = per_group * 3 * HEAD
    return pl.pallas_call(
        functools.partial(project_kernel, blocks=blocks, group=group, orders=orders, behind=len(behind)),
        out_shape=out_shape,
        in_specs=[pl.BlockSpec(memory_space=pltpu.SMEM)] + [any_space] * (blocks + 1 + len(behind)),
        out_specs=[pl.BlockSpec(memory_space=pltpu.VMEM)] * len(out_shape),
        scratch_shapes=[
            pltpu.VMEM((blocks, group_len, depth), BF16),
            pltpu.VMEM((depth, cols), BF16),
            pltpu.SemaphoreType.DMA((blocks,)),
            pltpu.SemaphoreType.DMA(()),
        ],
        compiler_params=pltpu.CompilerParams(vmem_limit_bytes=60 * MIB),
        cost_estimate=SMALL,
    )(meta, *x_blocks, weights, *behind)


def forward_kernel(*refs, parts, terms, behind):
    out_refs = refs[parts * terms + behind :]
    for p in range(parts):
        mine = refs[p * terms : (p + 1) * terms]
        out_refs[p][...] = sum(ref[...].astype(F32) for ref in mine).astype(BF16)


def forward(terms, behind):
    left = min(t.shape[0] for t in terms[0]) // 2
    shapes = [(left, *ts[0].shape[1:]) for ts in terms]
    specs = [pl.BlockSpec(shape, lambda i: (1, 0, 0)) for shape, ts in zip(shapes, terms) for _ in ts]
    return pl.pallas_call(
        functools.partial(forward_kernel, parts=len(terms), terms=len(terms[0]), behind=len(behind)),
        grid=(1,),
        out_shape=[jax.ShapeDtypeStruct(shape, BF16) for shape in shapes],
        in_specs=specs + [pl.BlockSpec(memory_space=pl.ANY)] * len(behind),
        out_specs=[pl.BlockSpec(shape, lambda i: (0, 0, 0)) for shape in shapes],
        compiler_params=pltpu.CompilerParams(vmem_limit_bytes=60 * MIB),
        cost_estimate=SMALL,
    )(*[t for ts in terms for t in ts], *behind)


def settle_kernel(bias_ref, scale_ref, *refs, parts, terms, behind):
    mine_ref, theirs_ref = refs[parts * terms + behind :]
    width = mine_ref.shape[2]
    head = 0
    for p in range(parts):
        for h in range(refs[p * terms].shape[2] // width):
            cols = pl.ds(h * width, width)
            for e, ref in enumerate((mine_ref, theirs_ref)):
                total = sum(t[e, :, cols].astype(F32) for t in refs[p * terms : (p + 1) * terms])
                ref[head] = ((total + bias_ref[head : head + 1, :]) * scale_ref[...]).astype(BF16)
            head += 1


def settle(terms, bias, scale, behind):
    heads, width = bias.shape
    rows = terms[0][0].shape[1]
    specs = [pl.BlockSpec((2, *t.shape[1:]), lambda i: (0, 0, 0)) for ts in terms for t in ts]
    whole = pl.BlockSpec((heads, rows, width), lambda i: (0, 0, 0))
    return pl.pallas_call(
        functools.partial(settle_kernel, parts=len(terms), terms=len(terms[0]), behind=len(behind)),
        grid=(1,),
        out_shape=[jax.ShapeDtypeStruct((heads, rows, width), BF16)] * 2,
        in_specs=[pl.BlockSpec((heads, width), lambda i: (0, 0)), pl.BlockSpec((1, width), lambda i: (0, 0))]
        + specs
        + [pl.BlockSpec(memory_space=pl.ANY)] * len(behind),
        out_specs=[whole, whole],
        compiler_params=pltpu.CompilerParams(vmem_limit_bytes=60 * MIB),
        cost_estimate=SMALL,
    )(bias, scale, *[t for ts in terms for t in ts], *behind)


def attend_kernel(meta_ref, own_ref, other_ref, k_ref, v_ref, *refs, key_len, behind):
    o_ref, nk_ref, nv_ref = refs[behind:]
    length = meta_ref[0]
    qkv = jnp.where(pl.program_id(0) < pl.num_programs(0) // 2, own_ref[0], other_ref[0])
    q, new_k, new_v = qkv[:, :HEAD], qkv[:, HEAD : 2 * HEAD], qkv[:, 2 * HEAD :]
    nk_ref[...] = new_k
    nv_ref[...] = new_v
    group = q.shape[0]
    cache_len = k_ref.shape[1]

    def scores_of(at):
        keys = k_ref[0, at : at + key_len, :]
        scores = lax.dot_general(q, keys, (((1,), (1,)), ((), ())), preferred_element_type=F32)
        positions = at + lax.broadcasted_iota(jnp.int32, (1, key_len), 1)
        return jnp.where(positions < length, scores, -1e30)

    def lane_sum(probs):
        total = probs[:, :HEAD]
        for at in range(HEAD, probs.shape[1], HEAD):
            total = total + probs[:, at : at + HEAD]
        return total

    rows = lax.broadcasted_iota(jnp.int32, (group, group), 0)
    cols = lax.broadcasted_iota(jnp.int32, (group, group), 1)
    scores = lax.dot_general(q, new_k, (((1,), (1,)), ((), ())), preferred_element_type=F32)
    scores = jnp.where(cols <= rows, scores, -1e30)
    following = scores_of(0)
    row_max = jnp.max(scores, axis=1, keepdims=True)
    probs = jnp.exp(scores - row_max)
    row_sum = lane_sum(probs)
    weighted = jnp.dot(probs.astype(BF16), new_v, preferred_element_type=F32)
    for at in range(0, cache_len, key_len):
        scores = following
        if at + key_len < cache_len:
            following = scores_of(at + key_len)
        new_max = jnp.maximum(row_max, jnp.max(scores, axis=1, keepdims=True))
        factor = jnp.exp(row_max - new_max)
        probs = jnp.exp(scores - new_max)
        row_max = new_max
        row_sum = row_sum * factor + lane_sum(probs)
        values = v_ref[0, at : at + key_len, :]
        weighted = weighted * factor + jnp.dot(probs.astype(BF16), values, preferred_element_type=F32)
    total = jnp.sum(row_sum, axis=1, keepdims=True)
    o_ref[...] = (weighted / total).astype(BF16)


def attend(meta, own, other, cache_k, cache_v, base, half, behind):
    count, group, width = own.shape
    heads = 2 * count
    cache_len = cache_k.shape[1]
    key_len = min(512, cache_len)

    def side(i, meta):
        return (i // count) ^ meta[1]

    cached = pl.BlockSpec((1, cache_len, HEAD), lambda i, meta: (0, 0, side(i, meta) * half + base + i % count))
    placed = pl.BlockSpec((group, HEAD), lambda i, meta: (0, side(i, meta) * count + i % count))
    return pl.pallas_call(
        functools.partial(attend_kernel, key_len=key_len, behind=len(behind)),
        out_shape=[jax.ShapeDtypeStruct((group, heads * HEAD), BF16)] * 3,
        grid_spec=pltpu.PrefetchScalarGridSpec(
            num_scalar_prefetch=1,
            grid=(heads,),
            in_specs=[
                pl.BlockSpec((1, group, width), lambda i, meta: (jnp.minimum(i, count - 1), 0, 0)),
                pl.BlockSpec((1, group, width), lambda i, meta: (jnp.maximum(i - count, 0), 0, 0)),
                cached,
                cached,
            ]
            + [pl.BlockSpec(memory_space=pl.ANY)] * len(behind),
            out_specs=[placed] * 3,
        ),
        compiler_params=pltpu.CompilerParams(vmem_limit_bytes=60 * MIB),
        cost_estimate=SMALL,
    )(meta, own, other, cache_k, cache_v, *behind)


def output_kernel(*refs, pairs, groups):
    a_refs = [refs[g * pairs : (g + 1) * pairs] for g in range(groups)]
    w_refs = refs[groups * pairs : groups * pairs + 2]
    out_refs, (buf, sem) = refs[groups * pairs + 2 : -2], refs[-2:]
    _, rows, head_cols = buf.shape
    half = head_cols // 2
    cols = half // groups
    chunk = rows // len(out_refs)
    for d in range(pairs):
        for g in range(groups):
            for side in range(2):
                pltpu.make_async_copy(
                    a_refs[g][d].at[:, pl.ds(side * cols, cols)],
                    buf.at[d, :, pl.ds(side * half + g * cols, cols)],
                    sem.at[d],
                ).start()
    for d in range(pairs):
        pltpu.make_async_copy(buf.at[d], buf.at[d], sem.at[d]).wait()
    for d in range(0, pairs, 2):
        tokens = buf[d : d + 2].reshape(2 * rows, head_cols)
        for j in range(2):
            product = jnp.dot(tokens, w_refs[j][...], preferred_element_type=F32).astype(BF16)
            for c, out_ref in enumerate(out_refs):
                for at in range(2):
                    first = at * rows + c * chunk
                    out_ref[j, d + at] = product[first : first + chunk]


def output(gathered, w_pair, chunks):
    groups, pairs = len(gathered), len(gathered[0])
    rows = gathered[0][0].shape[0]
    head_cols, out_cols = w_pair[0].shape
    space = pl.BlockSpec(memory_space=pl.ANY)
    vmem = pl.BlockSpec(memory_space=pltpu.VMEM)
    return pl.pallas_call(
        functools.partial(output_kernel, pairs=pairs, groups=groups),
        out_shape=[jax.ShapeDtypeStruct((2, pairs, rows // chunks, out_cols), BF16)] * chunks,
        in_specs=[space] * (groups * pairs) + [vmem] * 2,
        out_specs=[vmem] * chunks,
        scratch_shapes=[pltpu.VMEM((pairs, rows, head_cols), BF16), pltpu.SemaphoreType.DMA((pairs,))],
        compiler_params=pltpu.CompilerParams(vmem_limit_bytes=60 * MIB),
        cost_estimate=SMALL,
    )(*[a for part in gathered for a in part], *w_pair)


def block_call(kernel, out_shapes, scalars, arrays, shapes, indices, behind):
    return pl.pallas_call(
        functools.partial(kernel, behind=len(behind)),
        out_shape=[jax.ShapeDtypeStruct(shape, BF16) for shape in out_shapes],
        grid_spec=pltpu.PrefetchScalarGridSpec(
            num_scalar_prefetch=1,
            grid=(1,),
            in_specs=[pl.BlockSpec(shape, index) for shape, index in zip(shapes, indices)]
            + [pl.BlockSpec(memory_space=pl.ANY)] * len(behind),
            out_specs=[
                pl.BlockSpec(shape, lambda i, meta, rank=len(shape): (0,) * rank) for shape in out_shapes
            ],
        ),
        compiler_params=pltpu.CompilerParams(vmem_limit_bytes=60 * MIB),
        cost_estimate=SMALL,
    )(scalars, *arrays, *behind)


def split_pair_kernel(meta_ref, own_ref, came_ref, *refs, behind):
    mine_ref, sent_ref = refs[behind:]
    count = mine_ref.shape[1]
    pairs = 2 * count
    offsets = slots_in(2 * pairs, range(1, pairs.bit_length()))[::2]
    for at, e in enumerate(offsets):
        place = meta_ref[e]
        for j in range(2):
            block = jnp.where(place % 2 == 0, own_ref[j, place // 2], came_ref[1 - j, place // 2])
            if at < count:
                mine_ref[j, at] = block
            else:
                sent_ref[j, at - count] = block


def split_pair(places, own, came, behind):
    _, pairs, chunk, cols = own.shape
    first = lambda i, meta: (0, 0, 0, 0)
    shapes = [(2, pairs // 2, chunk, cols)] * 2
    return block_call(split_pair_kernel, shapes, places, [own, came], [own.shape] * 2, [first] * 2, behind)


def choose_kernel(meta_ref, keep_ref, came_ref, *refs, behind):
    mine_ref, sent_ref = refs[behind:]

    @pl.when(meta_ref[0] == 0)
    def _():
        mine_ref[...] = keep_ref[...]
        sent_ref[...] = came_ref[...]

    @pl.when(meta_ref[0] != 0)
    def _():
        mine_ref[...] = came_ref[...]
        sent_ref[...] = keep_ref[...]


def choose(flip, keep, came, behind):
    first = lambda i, meta: (0,) * keep.ndim
    return block_call(choose_kernel, [keep.shape] * 2, flip, [keep, came], [keep.shape] * 2, [first] * 2, behind)


def add_split_kernel(meta_ref, keep_ref, came_ref, *refs, behind):
    mine_ref, sent_ref = refs[behind:]
    count = mine_ref.shape[1]
    total = (keep_ref[...].astype(F32) + came_ref[...].astype(F32)).astype(BF16)
    mine_ref[...] = total[:, :count]
    sent_ref[...] = total[:, count:]


def add_split(keep, came, behind):
    slices, count, chunk, cols = keep.shape
    first = lambda i, meta: (0, 0, 0, 0)
    shapes = [(slices, count // 2, chunk, cols)] * 2
    scalars = jnp.zeros((1,), jnp.int32)
    return block_call(add_split_kernel, shapes, scalars, [keep, came], [keep.shape] * 2, [first] * 2, behind)


def finish_rows_kernel(meta_ref, keep_ref, came_ref, hidden_ref, bias_ref, *refs, behind):
    (out_ref,) = refs[behind:]
    cols = keep_ref.shape[3]
    total = [keep_ref[j, 0].astype(F32) + came_ref[j, 0].astype(F32) for j in range(2)]
    for side in range(2):
        at = pl.ds(side * cols, cols)
        part = jnp.where(meta_ref[0] == side, total[0], total[1])
        out_ref[:, at] = (part + bias_ref[:, at] + hidden_ref[:, at].astype(F32)).astype(BF16)


def finish_rows(meta, keep, came, hidden, bias, at, behind):
    chunk, cols = keep.shape[2:]
    width = 2 * cols
    shapes = [keep.shape, keep.shape, (chunk, width), (1, width)]
    first = lambda i, meta: (0, 0, 0, 0)
    indices = [first, first, lambda i, meta: (at, meta[1]), lambda i, meta: (0, 0)]
    arrays = [keep, came, hidden, bias[None]]
    return block_call(finish_rows_kernel, [(chunk, width)], meta, arrays, shapes, indices, behind)[0]


def local(
    rows_n,
    cols_n,
    hidden_in,
    norm_gain,
    norm_bias,
    w_query,
    w_keyval,
    bias_query,
    bias_keyval,
    cache_keys,
    cache_values,
    cache_lengths,
    owner_slot,
    w_out,
    bias_out,
):
    row = lax.axis_index("row")
    col = lax.axis_index("col")
    core = row & 1
    group_len, width = hidden_in.shape
    slice_len, head_cols = w_query.shape
    half = head_cols // HEAD // 2
    half_cols = head_cols // 2
    pairs = rows_n // 2
    row_bits = rows_n.bit_length() - 1
    col_bits = cols_n.bit_length() - 1
    q_scale = HEAD ** (-0.5)
    slot_ids = jnp.arange(rows_n, dtype=jnp.int32)
    is_owner = owner_slot[:, None] == slot_ids[None, :]
    inverse = jnp.sum(jnp.where(is_owner, slot_ids[:, None], 0), axis=0).astype(jnp.int32)

    pair = row // 2
    pieces = normalize(pair.reshape(1).astype(jnp.int32), hidden_in, norm_gain, norm_bias, pairs)
    x_blocks = [None] * rows_n
    for offset in reversed(range(pairs)):
        piece = swap(pieces[offset], "row", 2 * offset, rows_n) if offset else pieces[0]
        x_blocks[2 * offset] = piece

    groups = 3 if half % 3 == 0 else 1
    per_group = half // groups
    parts = [(g * per_group, (g + 1) * per_group) for g in range(groups)]
    taken = swap(w_query, "row", 1, rows_n), swap(w_keyval, "row", 1, rows_n)
    weights = weave(core, w_query, w_keyval, *taken, parts, [pieces[0]])
    w_pair = w_out, swap(fetch([w_out], [weights])[0], "row", 1, rows_n)
    arrived = fetch(x_blocks[2::2], [weights])
    for offset in range(pairs):
        x_blocks[2 * offset + 1] = swap(arrived[offset - 1] if offset else x_blocks[0], "row", 1, rows_n)

    bias = jnp.concatenate([bias_query[None], bias_keyval], axis=0).reshape(3, 2, half, HEAD).transpose(1, 2, 0, 3)
    bias = lax.dynamic_index_in_dim(bias, core, 0, keepdims=False).reshape(half, 3 * HEAD)
    scale = jnp.concatenate([jnp.full((HEAD,), q_scale, F32), jnp.ones((2 * HEAD,), F32)])

    counts = [per_group // 2, per_group - per_group // 2] if per_group > 1 else [1]
    pair_bits = list(range(1, row_bits))
    orders = [pair_bits[at % len(pair_bits) :] + pair_bits[: at % len(pair_bits)] for at in range(len(counts))]
    project_meta = (inverse[row ^ slot_ids] ^ row).astype(jnp.int32)
    attend_meta = jnp.stack([cache_lengths[inverse[row]], core]).astype(jnp.int32)

    def project_group(g, behind):
        return project(project_meta, x_blocks, weights, g, per_group, orders, counts, behind)

    projected = [project_group(0, [])]
    key_parts, value_parts, gathered, finished, waiting = [], [], [], [], []

    def finish(g):
        base = g * per_group
        mine, theirs = settle(
            waiting[g],
            bias[base : base + per_group],
            scale[None],
            finished[-1:] + ([projected[g + 2][0]] if g + 2 < groups else []),
        )
        came = swap(theirs, "row", 1, rows_n)
        attended, new_k, new_v = attend(
            attend_meta, mine, came, cache_keys, cache_values, base, half, []
        )
        finished.append(attended)
        key_parts.append(new_k)
        value_parts.append(new_v)
        gathered.append([swap(attended, "row", 2 * d, rows_n) if d else attended for d in range(pairs)])

    for g in range(groups):
        terms = [[projected[g][2 * p]] for p in range(len(orders))]
        sends = [projected[g][2 * p + 1] for p in range(len(orders))]
        if g + 1 < groups:
            projected.append(project_group(g + 1, [sent] if g else [projected[0][0], w_pair[1]]))
        for at in range(len(pair_bits)):
            for p, order in enumerate(orders):
                terms[p].append(swap(sends[p], "row", 1 << order[at], rows_n))
            if at + 1 < len(pair_bits):
                sends = forward(terms, finished[-1:] + ([projected[g + 1][0]] if g + 1 < groups else []))
                sent = sends[0]
        waiting.append(terms)
        if g:
            finish(g - 1)
    finish(groups - 1)

    cols = per_group * HEAD
    new_k, new_v = (
        jnp.concatenate([p[:, side * cols : (side + 1) * cols] for side in range(2) for p in parts], axis=1)[None]
        for parts in (key_parts, value_parts)
    )

    places = (owner_slot[row ^ slot_ids] ^ row).astype(jnp.int32)
    shift = row_bits - col_bits
    if shift != 1:
        raise ValueError("unexpected mesh")
    chunks = 4
    chunk = group_len // chunks
    last = row_bits - 1
    flips = [((row >> bit) ^ (col >> (bit - 1))) & 1 for bit in range(1, row_bits)]
    flips = [flip.reshape(1).astype(jnp.int32) for flip in flips]
    final_meta = jnp.stack([core, col]).astype(jnp.int32)
    late = [0, 0] + [at for bit in range(1, last) for at in (4.5 * bit + 1.5, 4.5 * bit + 4.5)]
    late += [4.5 * last + 1.5, 4.5 * last + 2.8]
    order = sorted((c * (2 if step > 1 else 0.5) + late[step], step, c) for c in range(chunks) for step in range(1, 2 * last + 2))
    products = output(gathered, w_pair, chunks)
    state = {c: (product, swap(product, "row", 1, rows_n)) for c, product in enumerate(products)}
    done, order_behind = {}, []
    for _, step, c in order:
        if step == 2 * last + 1:
            done[c] = finish_rows(final_meta, *state[c], hidden_in, bias_out, c, order_behind)
            order_behind = [done[c]]
        else:
            bit = (step + 1) // 2
            if step == 1:
                keep, sent = split_pair(places, *state[c], order_behind)
            elif step % 2:
                keep, sent = add_split(*state[c], order_behind)
            else:
                keep, sent = choose(flips[bit - 1], *state[c], order_behind)
            axis, mask, size = ("row", 1 << bit, rows_n) if step % 2 else ("col", 1 << (bit - 1), cols_n)
            state[c] = (keep, swap(sent, axis, mask, size))
            order_behind = [sent]
    hidden_out = jnp.concatenate([done[c] for c in range(chunks)], axis=0)
    return hidden_out, new_k, new_v


def solution(mesh):
    placed = (
        P("row", None),
        P(),
        P(),
        P("row", "col"),
        P("row", None, "col"),
        P("col"),
        P(None, "col"),
        P("row", None, "col"),
        P("row", None, "col"),
        P(),
        P(),
        P("col", "row"),
        P("col"),
    )
    return jax.shard_map(
        functools.partial(local, mesh.shape["row"], mesh.shape["col"]),
        mesh=mesh,
        in_specs=placed,
        out_specs=(P("row", "col"), P("row", None, "col"), P("row", None, "col")),
        check_vma=False,
    )
```

```python
import functools

import jax
import jax.numpy as jnp
from jax import lax
from jax.experimental import pallas as pl
from jax.experimental.pallas import tpu as pltpu
from jax.sharding import PartitionSpec as P

HEAD = 128
F32 = jnp.float32
MIB = 1024 * 1024
SMALL = pl.CostEstimate(flops=1, bytes_accessed=1, transcendentals=0)
BF16 = jnp.bfloat16


def normalize_kernel(meta_ref, hidden_ref, gain_ref, bias_ref, *out_refs):
    piece_refs = out_refs
    width = hidden_ref.shape[1]
    length = piece_refs[0].shape[1]
    rows = hidden_ref[...].astype(F32)
    mean = jnp.sum(rows, axis=1, keepdims=True) / width
    centered = rows - mean
    var = jnp.sum(centered * centered, axis=1, keepdims=True) / width
    factor = lax.rsqrt(var + 1e-05)
    for d, ref in enumerate(piece_refs):
        part = pl.ds(pl.multiple_of((meta_ref[0] ^ d) * length, HEAD), length)
        ref[...] = ((hidden_ref[:, part].astype(F32) - mean) * factor * gain_ref[:, part] + bias_ref[:, part]).astype(BF16)


def normalize(meta, hidden, gain, bias, pairs):
    rows, width = hidden.shape
    step = 32
    whole = pl.BlockSpec((1, width), lambda i, meta: (0, 0))
    return pl.pallas_call(
        normalize_kernel,
        out_shape=[jax.ShapeDtypeStruct((rows, width // pairs), BF16)] * pairs,
        grid_spec=pltpu.PrefetchScalarGridSpec(
            num_scalar_prefetch=1,
            grid=(rows // step,),
            in_specs=[pl.BlockSpec((step, width), lambda i, meta: (i, 0)), whole, whole],
            out_specs=[pl.BlockSpec((step, width // pairs), lambda i, meta: (i, 0))] * pairs,
        ),
        compiler_params=pltpu.CompilerParams(vmem_limit_bytes=60 * MIB),
        cost_estimate=SMALL,
    )(meta, hidden, gain[None], bias[None])


def weave_kernel(meta_ref, q_ref, kv_ref, taken_q_ref, taken_kv_ref, *refs, cuts, behind):
    (out_ref,) = refs[behind:]

    def weave(queries_ref, keyval_ref):
        at = 0
        for first, last in cuts:
            for kind in range(3):
                cols = pl.ds(first * HEAD, (last - first) * HEAD)
                part = queries_ref[:, cols] if kind == 0 else keyval_ref[:, kind - 1, cols]
                out_ref[:, pl.ds(at, (last - first) * HEAD)] = part
                at += (last - first) * HEAD

    @pl.when(pl.program_id(0) == 0)
    def _():
        weave(q_ref, kv_ref)

    @pl.when(pl.program_id(0) != 0)
    def _():
        weave(taken_q_ref, taken_kv_ref)


def weave(core, w_query, w_keyval, taken_query, taken_keyval, cuts, behind):
    rows, cols = w_query.shape
    half = cols // 2
    step = 128 if rows % 128 == 0 else 64
    steps = rows // step
    own = lambda side, i, meta: jnp.where(side == 0, i, steps - 1)
    other = lambda side, i, meta: jnp.where(side == 0, 0, i)
    specs = []
    for place in (own, other):
        specs.append(pl.BlockSpec((step, half), lambda side, i, meta, place=place: (place(side, i, meta), meta[0])))
        specs.append(pl.BlockSpec((step, 2, half), lambda side, i, meta, place=place: (place(side, i, meta), 0, meta[0])))
    return pl.pallas_call(
        functools.partial(weave_kernel, cuts=cuts, behind=len(behind)),
        out_shape=jax.ShapeDtypeStruct((2 * rows, 3 * half), BF16),
        grid_spec=pltpu.PrefetchScalarGridSpec(
            num_scalar_prefetch=1,
            grid=(2, steps),
            in_specs=specs + [pl.BlockSpec(memory_space=pl.ANY)] * len(behind),
            out_specs=pl.BlockSpec((step, 3 * half), lambda side, i, meta: ((meta[0] ^ side) * steps + i, 0)),
        ),
        compiler_params=pltpu.CompilerParams(vmem_limit_bytes=60 * MIB),
        cost_estimate=SMALL,
    )(core.reshape(1).astype(jnp.int32), w_query, w_keyval, taken_query, taken_keyval, *behind)


def fetch_kernel(*refs, count, behind):
    out_refs, sem = refs[count + behind : -1], refs[-1]
    copies = [pltpu.make_async_copy(refs[at], out_refs[at], sem.at[at]) for at in range(count)]
    for copy in copies:
        copy.start()
    for copy in copies:
        copy.wait()


def fetch(sources, behind):
    space = pl.BlockSpec(memory_space=pl.ANY)
    return pl.pallas_call(
        functools.partial(fetch_kernel, count=len(sources), behind=len(behind)),
        out_shape=[jax.ShapeDtypeStruct(source.shape, source.dtype) for source in sources],
        in_specs=[space] * (len(sources) + len(behind)),
        out_specs=[pl.BlockSpec(memory_space=pltpu.VMEM)] * len(sources),
        scratch_shapes=[pltpu.SemaphoreType.DMA((len(sources),))],
        compiler_params=pltpu.CompilerParams(vmem_limit_bytes=60 * MIB),
        cost_estimate=SMALL,
    )(*sources, *behind)


def swap(value, axis, mask, size):
    return lax.ppermute(value, axis, [(i, i ^ mask) for i in range(size)])


def gather_block(table, places, dst, sem):
    for at, place in enumerate(places):

        @pl.when(table == at)
        def _(place=place):
            pltpu.make_async_copy(place, dst, sem).start()


def project_kernel(meta_ref, *refs, blocks, group, orders, behind):
    x_refs, w_ref = refs[:blocks], refs[blocks]
    out_refs, (x_buf, w_buf, x_sem, w_sem) = refs[blocks + 1 + behind : -4], refs[-4:]
    cols = w_buf.shape[1] // 3
    load = pltpu.make_async_copy(w_ref.at[:, pl.ds(group * 3 * cols, 3 * cols)], w_buf, w_sem)
    load.start()
    sequence = sorted(range(blocks), key=lambda e: -sum(bool(e >> order[0] & 1) for order in orders))
    for at, e in enumerate(sequence):
        gather_block(meta_ref[e], x_refs, x_buf.at[at], x_sem.at[at])
    load.wait()
    group_len = x_buf.shape[1]
    batch = 2
    for start in range(0, blocks, batch):
        for at in range(start, start + batch):
            pltpu.make_async_copy(x_refs[0], x_buf.at[at], x_sem.at[at]).wait()
        tokens = x_buf[start : start + batch].reshape(batch * group_len, x_buf.shape[2])
        product = jnp.dot(tokens, w_buf[...], preferred_element_type=F32).astype(BF16)
        first = 0
        for p, order in enumerate(orders):
            keep_ref, send_ref = out_refs[2 * p], out_refs[2 * p + 1]
            count = keep_ref.shape[2] // (3 * HEAD)
            ranked = slots_in(blocks, order)
            for c in range(batch):
                place = ranked.index(sequence[start + c])
                ref = keep_ref if place < blocks // 2 else send_ref
                for h in range(count):
                    for kind in range(3):
                        at = kind * cols + (first + h) * HEAD
                        ref[place % (blocks // 2), :, pl.ds((3 * h + kind) * HEAD, HEAD)] = product[
                            c * group_len : (c + 1) * group_len, at : at + HEAD
                        ]
            first += count


def slots_in(blocks, order):
    return sorted(range(blocks), key=lambda e: [e >> bit & 1 for bit in order] + [e & 1])


def project(meta, x_blocks, weights, group, per_group, orders, counts, behind):
    blocks = len(x_blocks)
    group_len, depth = x_blocks[0].shape
    any_space = pl.BlockSpec(memory_space=pl.ANY)
    out_shape = []
    for count in counts:
        out_shape += [jax.ShapeDtypeStruct((blocks // 2, group_len, count * 3 * HEAD), BF16)] * 2
    cols = per_group * 3 * HEAD
    return pl.pallas_call(
        functools.partial(project_kernel, blocks=blocks, group=group, orders=orders, behind=len(behind)),
        out_shape=out_shape,
        in_specs=[pl.BlockSpec(memory_space=pltpu.SMEM)] + [any_space] * (blocks + 1 + len(behind)),
        out_specs=[pl.BlockSpec(memory_space=pltpu.VMEM)] * len(out_shape),
        scratch_shapes=[
            pltpu.VMEM((blocks, group_len, depth), BF16),
            pltpu.VMEM((depth, cols), BF16),
            pltpu.SemaphoreType.DMA((blocks,)),
            pltpu.SemaphoreType.DMA(()),
        ],
        compiler_params=pltpu.CompilerParams(vmem_limit_bytes=48 * MIB),
        cost_estimate=SMALL,
    )(meta, *x_blocks, weights, *behind)


def forward_kernel(*refs, parts, terms, behind):
    out_refs = refs[parts * terms + behind :]
    for p in range(parts):
        mine = refs[p * terms : (p + 1) * terms]
        out_refs[p][...] = sum(ref[...].astype(F32) for ref in mine).astype(BF16)


def forward(terms, behind):
    left = min(t.shape[0] for t in terms[0]) // 2
    shapes = [(left, *ts[0].shape[1:]) for ts in terms]
    specs = [pl.BlockSpec(shape, lambda i: (1, 0, 0)) for shape, ts in zip(shapes, terms) for _ in ts]
    return pl.pallas_call(
        functools.partial(forward_kernel, parts=len(terms), terms=len(terms[0]), behind=len(behind)),
        grid=(1,),
        out_shape=[jax.ShapeDtypeStruct(shape, BF16) for shape in shapes],
        in_specs=specs + [pl.BlockSpec(memory_space=pl.ANY)] * len(behind),
        out_specs=[pl.BlockSpec(shape, lambda i: (0, 0, 0)) for shape in shapes],
        compiler_params=pltpu.CompilerParams(vmem_limit_bytes=60 * MIB),
        cost_estimate=SMALL,
    )(*[t for ts in terms for t in ts], *behind)


def settle_kernel(bias_ref, scale_ref, *refs, parts, terms, behind):
    mine_ref, theirs_ref = refs[parts * terms + behind :]
    width = mine_ref.shape[2]
    head = 0
    for p in range(parts):
        for h in range(refs[p * terms].shape[2] // width):
            cols = pl.ds(h * width, width)
            for e, ref in enumerate((mine_ref, theirs_ref)):
                total = sum(t[e, :, cols].astype(F32) for t in refs[p * terms : (p + 1) * terms])
                ref[head] = ((total + bias_ref[head : head + 1, :]) * scale_ref[...]).astype(BF16)
            head += 1


def settle(terms, bias, scale, behind):
    heads, width = bias.shape
    rows = terms[0][0].shape[1]
    specs = [pl.BlockSpec((2, *t.shape[1:]), lambda i: (0, 0, 0)) for ts in terms for t in ts]
    whole = pl.BlockSpec((heads, rows, width), lambda i: (0, 0, 0))
    return pl.pallas_call(
        functools.partial(settle_kernel, parts=len(terms), terms=len(terms[0]), behind=len(behind)),
        grid=(1,),
        out_shape=[jax.ShapeDtypeStruct((heads, rows, width), BF16)] * 2,
        in_specs=[pl.BlockSpec((heads, width), lambda i: (0, 0)), pl.BlockSpec((1, width), lambda i: (0, 0))]
        + specs
        + [pl.BlockSpec(memory_space=pl.ANY)] * len(behind),
        out_specs=[whole, whole],
        compiler_params=pltpu.CompilerParams(vmem_limit_bytes=60 * MIB),
        cost_estimate=SMALL,
    )(bias, scale, *[t for ts in terms for t in ts], *behind)


def attend_kernel(meta_ref, own_ref, other_ref, k_ref, v_ref, *refs, key_len, behind):
    o_ref, nk_ref, nv_ref = refs[behind:]
    length = meta_ref[0]
    qkv = jnp.where(pl.program_id(0) < pl.num_programs(0) // 2, own_ref[0], other_ref[0])
    q, new_k, new_v = qkv[:, :HEAD], qkv[:, HEAD : 2 * HEAD], qkv[:, 2 * HEAD :]
    nk_ref[...] = new_k
    nv_ref[...] = new_v
    group = q.shape[0]
    cache_len = k_ref.shape[1]

    def scores_of(at):
        keys = k_ref[0, at : at + key_len, :]
        scores = lax.dot_general(q, keys, (((1,), (1,)), ((), ())), preferred_element_type=F32)
        positions = at + lax.broadcasted_iota(jnp.int32, (1, key_len), 1)
        return jnp.where(positions < length, scores, -1e30)

    def lane_sum(probs):
        total = probs[:, :HEAD]
        for at in range(HEAD, probs.shape[1], HEAD):
            total = total + probs[:, at : at + HEAD]
        return total

    rows = lax.broadcasted_iota(jnp.int32, (group, group), 0)
    cols = lax.broadcasted_iota(jnp.int32, (group, group), 1)
    scores = lax.dot_general(q, new_k, (((1,), (1,)), ((), ())), preferred_element_type=F32)
    scores = jnp.where(cols <= rows, scores, -1e30)
    following = scores_of(0)
    row_max = jnp.max(scores, axis=1, keepdims=True)
    probs = jnp.exp(scores - row_max)
    row_sum = lane_sum(probs)
    weighted = jnp.dot(probs.astype(BF16), new_v, preferred_element_type=F32)
    for at in range(0, cache_len, key_len):
        scores = following
        if at + key_len < cache_len:
            following = scores_of(at + key_len)
        new_max = jnp.maximum(row_max, jnp.max(scores, axis=1, keepdims=True))
        factor = jnp.exp(row_max - new_max)
        probs = jnp.exp(scores - new_max)
        row_max = new_max
        row_sum = row_sum * factor + lane_sum(probs)
        values = v_ref[0, at : at + key_len, :]
        weighted = weighted * factor + jnp.dot(probs.astype(BF16), values, preferred_element_type=F32)
    total = jnp.sum(row_sum, axis=1, keepdims=True)
    o_ref[...] = (weighted / total).astype(BF16)


def attend(meta, own, other, cache_k, cache_v, base, half, behind):
    count, group, width = own.shape
    heads = 2 * count
    cache_len = cache_k.shape[1]
    key_len = min(512, cache_len)

    def side(i, meta):
        return (i // count) ^ meta[1]

    cached = pl.BlockSpec((1, cache_len, HEAD), lambda i, meta: (0, 0, side(i, meta) * half + base + i % count))
    placed = pl.BlockSpec((group, HEAD), lambda i, meta: (0, side(i, meta) * count + i % count))
    return pl.pallas_call(
        functools.partial(attend_kernel, key_len=key_len, behind=len(behind)),
        out_shape=[jax.ShapeDtypeStruct((group, heads * HEAD), BF16)] * 3,
        grid_spec=pltpu.PrefetchScalarGridSpec(
            num_scalar_prefetch=1,
            grid=(heads,),
            in_specs=[
                pl.BlockSpec((1, group, width), lambda i, meta: (jnp.minimum(i, count - 1), 0, 0)),
                pl.BlockSpec((1, group, width), lambda i, meta: (jnp.maximum(i - count, 0), 0, 0)),
                cached,
                cached,
            ]
            + [pl.BlockSpec(memory_space=pl.ANY)] * len(behind),
            out_specs=[placed] * 3,
        ),
        compiler_params=pltpu.CompilerParams(vmem_limit_bytes=60 * MIB),
        cost_estimate=SMALL,
    )(meta, own, other, cache_k, cache_v, *behind)


def output_kernel(*refs, pairs, groups):
    a_refs = [refs[g * pairs : (g + 1) * pairs] for g in range(groups)]
    w_refs = refs[groups * pairs : groups * pairs + 2]
    out_refs, (buf, sem) = refs[groups * pairs + 2 : -2], refs[-2:]
    _, rows, head_cols = buf.shape
    half = head_cols // 2
    cols = half // groups
    chunk = rows // len(out_refs)
    for d in range(pairs):
        for g in range(groups):
            for side in range(2):
                pltpu.make_async_copy(
                    a_refs[g][d].at[:, pl.ds(side * cols, cols)],
                    buf.at[d, :, pl.ds(side * half + g * cols, cols)],
                    sem.at[d],
                ).start()
    for d in range(pairs):
        pltpu.make_async_copy(buf.at[d], buf.at[d], sem.at[d]).wait()
    for d in range(0, pairs, 2):
        tokens = buf[d : d + 2].reshape(2 * rows, head_cols)
        for j in range(2):
            product = jnp.dot(tokens, w_refs[j][...], preferred_element_type=F32).astype(BF16)
            for c, out_ref in enumerate(out_refs):
                for at in range(2):
                    first = at * rows + c * chunk
                    out_ref[j, d + at] = product[first : first + chunk]


def output(gathered, w_pair, chunks):
    groups, pairs = len(gathered), len(gathered[0])
    rows = gathered[0][0].shape[0]
    head_cols, out_cols = w_pair[0].shape
    space = pl.BlockSpec(memory_space=pl.ANY)
    vmem = pl.BlockSpec(memory_space=pltpu.VMEM)
    return pl.pallas_call(
        functools.partial(output_kernel, pairs=pairs, groups=groups),
        out_shape=[jax.ShapeDtypeStruct((2, pairs, rows // chunks, out_cols), BF16)] * chunks,
        in_specs=[space] * (groups * pairs) + [vmem] * 2,
        out_specs=[vmem] * chunks,
        scratch_shapes=[pltpu.VMEM((pairs, rows, head_cols), BF16), pltpu.SemaphoreType.DMA((pairs,))],
        compiler_params=pltpu.CompilerParams(vmem_limit_bytes=40 * MIB),
        cost_estimate=SMALL,
    )(*[a for part in gathered for a in part], *w_pair)


def block_call(kernel, out_shapes, scalars, arrays, shapes, indices, behind):
    return pl.pallas_call(
        functools.partial(kernel, behind=len(behind)),
        out_shape=[jax.ShapeDtypeStruct(shape, BF16) for shape in out_shapes],
        grid_spec=pltpu.PrefetchScalarGridSpec(
            num_scalar_prefetch=1,
            grid=(1,),
            in_specs=[pl.BlockSpec(shape, index) for shape, index in zip(shapes, indices)]
            + [pl.BlockSpec(memory_space=pl.ANY)] * len(behind),
            out_specs=[
                pl.BlockSpec(shape, lambda i, meta, rank=len(shape): (0,) * rank) for shape in out_shapes
            ],
        ),
        compiler_params=pltpu.CompilerParams(vmem_limit_bytes=16 * MIB),
        cost_estimate=SMALL,
    )(scalars, *arrays, *behind)


def split_pair_kernel(meta_ref, own_ref, came_ref, *refs, behind):
    mine_ref, sent_ref = refs[behind:]
    count = mine_ref.shape[1]
    pairs = 2 * count
    offsets = slots_in(2 * pairs, range(1, pairs.bit_length()))[::2]
    for at, e in enumerate(offsets):
        place = meta_ref[e]
        for j in range(2):
            block = jnp.where(place % 2 == 0, own_ref[j, place // 2], came_ref[1 - j, place // 2])
            if at < count:
                mine_ref[j, at] = block
            else:
                sent_ref[j, at - count] = block


def split_pair(places, own, came, behind):
    _, pairs, chunk, cols = own.shape
    first = lambda i, meta: (0, 0, 0, 0)
    shapes = [(2, pairs // 2, chunk, cols)] * 2
    return block_call(split_pair_kernel, shapes, places, [own, came], [own.shape] * 2, [first] * 2, behind)


def choose_kernel(meta_ref, keep_ref, came_ref, *refs, behind):
    mine_ref, sent_ref = refs[behind:]

    @pl.when(meta_ref[0] == 0)
    def _():
        mine_ref[...] = keep_ref[...]
        sent_ref[...] = came_ref[...]

    @pl.when(meta_ref[0] != 0)
    def _():
        mine_ref[...] = came_ref[...]
        sent_ref[...] = keep_ref[...]


def choose(flip, keep, came, behind):
    first = lambda i, meta: (0,) * keep.ndim
    return block_call(choose_kernel, [keep.shape] * 2, flip, [keep, came], [keep.shape] * 2, [first] * 2, behind)


def add_split_kernel(meta_ref, keep_ref, came_ref, *refs, behind):
    mine_ref, sent_ref = refs[behind:]
    count = mine_ref.shape[1]
    total = (keep_ref[...].astype(F32) + came_ref[...].astype(F32)).astype(BF16)
    mine_ref[...] = total[:, :count]
    sent_ref[...] = total[:, count:]


def add_split(keep, came, behind):
    slices, count, chunk, cols = keep.shape
    first = lambda i, meta: (0, 0, 0, 0)
    shapes = [(slices, count // 2, chunk, cols)] * 2
    scalars = jnp.zeros((1,), jnp.int32)
    return block_call(add_split_kernel, shapes, scalars, [keep, came], [keep.shape] * 2, [first] * 2, behind)


def finish_rows_kernel(meta_ref, keep_ref, came_ref, hidden_ref, bias_ref, *refs, behind):
    (out_ref,) = refs[behind:]
    cols = keep_ref.shape[3]
    total = [keep_ref[j, 0].astype(F32) + came_ref[j, 0].astype(F32) for j in range(2)]
    for side in range(2):
        at = pl.ds(side * cols, cols)
        part = jnp.where(meta_ref[0] == side, total[0], total[1])
        out_ref[:, at] = (part + bias_ref[:, at] + hidden_ref[:, at].astype(F32)).astype(BF16)


def finish_rows(meta, keep, came, hidden, bias, at, behind):
    chunk, cols = keep.shape[2:]
    width = 2 * cols
    shapes = [keep.shape, keep.shape, (chunk, width), (1, width)]
    first = lambda i, meta: (0, 0, 0, 0)
    indices = [first, first, lambda i, meta: (at, meta[1]), lambda i, meta: (0, 0)]
    arrays = [keep, came, hidden, bias[None]]
    return block_call(finish_rows_kernel, [(chunk, width)], meta, arrays, shapes, indices, behind)[0]


def local(
    rows_n,
    cols_n,
    hidden_in,
    norm_gain,
    norm_bias,
    w_query,
    w_keyval,
    bias_query,
    bias_keyval,
    cache_keys,
    cache_values,
    cache_lengths,
    owner_slot,
    w_out,
    bias_out,
):
    row = lax.axis_index("row")
    col = lax.axis_index("col")
    core = row & 1
    group_len, width = hidden_in.shape
    slice_len, head_cols = w_query.shape
    half = head_cols // HEAD // 2
    half_cols = head_cols // 2
    pairs = rows_n // 2
    row_bits = rows_n.bit_length() - 1
    col_bits = cols_n.bit_length() - 1
    q_scale = HEAD ** (-0.5)
    slot_ids = jnp.arange(rows_n, dtype=jnp.int32)
    is_owner = owner_slot[:, None] == slot_ids[None, :]
    inverse = jnp.sum(jnp.where(is_owner, slot_ids[:, None], 0), axis=0).astype(jnp.int32)

    pair = row // 2
    pieces = normalize(pair.reshape(1).astype(jnp.int32), hidden_in, norm_gain, norm_bias, pairs)
    x_blocks = [None] * rows_n
    for offset in reversed(range(pairs)):
        piece = swap(pieces[offset], "row", 2 * offset, rows_n) if offset else pieces[0]
        x_blocks[2 * offset] = piece

    groups = 3 if half % 3 == 0 else 1
    per_group = half // groups
    parts = [(g * per_group, (g + 1) * per_group) for g in range(groups)]
    taken = swap(w_query, "row", 1, rows_n), swap(w_keyval, "row", 1, rows_n)
    weights = weave(core, w_query, w_keyval, *taken, parts, [pieces[0]])
    *arrived, w_given = fetch([*x_blocks[::2], w_out], [weights])
    for offset in range(pairs):
        x_blocks[2 * offset + 1] = swap(arrived[offset], "row", 1, rows_n)
    w_pair = w_out, swap(w_given, "row", 1, rows_n)

    bias = jnp.concatenate([bias_query[None], bias_keyval], axis=0).reshape(3, 2, half, HEAD).transpose(1, 2, 0, 3)
    bias = lax.dynamic_index_in_dim(bias, core, 0, keepdims=False).reshape(half, 3 * HEAD)
    scale = jnp.concatenate([jnp.full((HEAD,), q_scale, F32), jnp.ones((2 * HEAD,), F32)])

    counts = [per_group // 2, per_group - per_group // 2] if per_group > 1 else [1]
    pair_bits = list(range(1, row_bits))
    orders = [pair_bits[at % len(pair_bits) :] + pair_bits[: at % len(pair_bits)] for at in range(len(counts))]
    project_meta = (inverse[row ^ slot_ids] ^ row).astype(jnp.int32)
    attend_meta = jnp.stack([cache_lengths[inverse[row]], core]).astype(jnp.int32)

    def project_group(g, behind):
        return project(project_meta, x_blocks, weights, g, per_group, orders, counts, behind)

    projected = [project_group(0, [])]
    key_parts, value_parts, gathered, finished, waiting = [], [], [], [], []

    def finish(g):
        base = g * per_group
        mine, theirs = settle(
            waiting[g],
            bias[base : base + per_group],
            scale[None],
            finished[-1:] + ([projected[g + 2][0]] if g + 2 < groups else [])
            + ([sent] if g + 1 < groups else []),
        )
        came = swap(theirs, "row", 1, rows_n)
        attended, new_k, new_v = attend(
            attend_meta, mine, came, cache_keys, cache_values, base, half, []
        )
        finished.append(attended)
        key_parts.append(new_k)
        value_parts.append(new_v)
        gathered.append([swap(attended, "row", 2 * d, rows_n) if d else attended for d in range(pairs)])

    for g in range(groups):
        terms = [[projected[g][2 * p]] for p in range(len(orders))]
        sends = [projected[g][2 * p + 1] for p in range(len(orders))]
        if g + 1 < groups:
            projected.append(project_group(g + 1, [sent] if g else [projected[0][0], w_pair[1]]))
        for at in range(len(pair_bits)):
            for p, order in enumerate(orders):
                terms[p].append(swap(sends[p], "row", 1 << order[at], rows_n))
            if at + 1 < len(pair_bits):
                sends = forward(terms, finished[-1:] + ([projected[g + 1][0]] if g + 1 < groups else []))
                sent = sends[0]
        waiting.append(terms)
        if g:
            finish(g - 1)
    finish(groups - 1)

    cols = per_group * HEAD
    new_k, new_v = (
        jnp.concatenate([p[:, side * cols : (side + 1) * cols] for side in range(2) for p in parts], axis=1)[None]
        for parts in (key_parts, value_parts)
    )

    places = (owner_slot[row ^ slot_ids] ^ row).astype(jnp.int32)
    shift = row_bits - col_bits
    if shift != 1:
        raise ValueError("unexpected mesh")
    chunks = 4
    chunk = group_len // chunks
    last = row_bits - 1
    flips = [((row >> bit) ^ (col >> (bit - 1))) & 1 for bit in range(1, row_bits)]
    flips = [flip.reshape(1).astype(jnp.int32) for flip in flips]
    final_meta = jnp.stack([core, col]).astype(jnp.int32)
    late = [0, 0] + [at for bit in range(1, last) for at in (4.5 * bit + 1.5, 4.5 * bit + 4.5)]
    late += [4.5 * last + 1.5, 4.5 * last + 2.8]
    order = sorted((c * (2 if step > 1 else 0.5) + late[step], step, c) for c in range(chunks) for step in range(1, 2 * last + 2))
    products = output(gathered, w_pair, chunks)
    state = {c: (product, swap(product, "row", 1, rows_n)) for c, product in enumerate(products)}
    done, order_behind = {}, []
    for _, step, c in order:
        if step == 2 * last + 1:
            done[c] = finish_rows(final_meta, *state[c], hidden_in, bias_out, c, order_behind)
            order_behind = [done[c]]
        else:
            bit = (step + 1) // 2
            if step == 1:
                keep, sent = split_pair(places, *state[c], order_behind)
            elif step % 2:
                keep, sent = add_split(*state[c], order_behind)
            else:
                keep, sent = choose(flips[bit - 1], *state[c], order_behind)
            axis, mask, size = ("row", 1 << bit, rows_n) if step % 2 else ("col", 1 << (bit - 1), cols_n)
            state[c] = (keep, swap(sent, axis, mask, size))
            order_behind = [sent]
    hidden_out = jnp.concatenate([done[c] for c in range(chunks)], axis=0)
    return hidden_out, new_k, new_v


def solution(mesh):
    placed = (
        P("row", None),
        P(),
        P(),
        P("row", "col"),
        P("row", None, "col"),
        P("col"),
        P(None, "col"),
        P("row", None, "col"),
        P("row", None, "col"),
        P(),
        P(),
        P("col", "row"),
        P("col"),
    )
    return jax.shard_map(
        functools.partial(local, mesh.shape["row"], mesh.shape["col"]),
        mesh=mesh,
        in_specs=placed,
        out_specs=(P("row", "col"), P("row", None, "col"), P("row", None, "col")),
        check_vma=False,
    )
```

```python
import functools

import jax
import jax.numpy as jnp
from jax import lax
from jax.experimental import pallas as pl
from jax.experimental.pallas import tpu as pltpu
from jax.sharding import PartitionSpec as P

HEAD = 128
F32 = jnp.float32
MIB = 1024 * 1024
SMALL = pl.CostEstimate(flops=1, bytes_accessed=1, transcendentals=0)
BF16 = jnp.bfloat16


def normalize_kernel(meta_ref, hidden_ref, gain_ref, bias_ref, *out_refs):
    piece_refs = out_refs
    width = hidden_ref.shape[1]
    length = piece_refs[0].shape[1]
    rows = hidden_ref[...].astype(F32)
    mean = jnp.sum(rows, axis=1, keepdims=True) / width
    centered = rows - mean
    var = jnp.sum(centered * centered, axis=1, keepdims=True) / width
    factor = lax.rsqrt(var + 1e-05)
    for d, ref in enumerate(piece_refs):
        part = pl.ds(pl.multiple_of((meta_ref[0] ^ d) * length, HEAD), length)
        ref[...] = ((hidden_ref[:, part].astype(F32) - mean) * factor * gain_ref[:, part] + bias_ref[:, part]).astype(BF16)


def normalize(meta, hidden, gain, bias, pairs):
    rows, width = hidden.shape
    step = 32
    whole = pl.BlockSpec((1, width), lambda i, meta: (0, 0))
    return pl.pallas_call(
        normalize_kernel,
        out_shape=[jax.ShapeDtypeStruct((rows, width // pairs), BF16)] * pairs,
        grid_spec=pltpu.PrefetchScalarGridSpec(
            num_scalar_prefetch=1,
            grid=(rows // step,),
            in_specs=[pl.BlockSpec((step, width), lambda i, meta: (i, 0)), whole, whole],
            out_specs=[pl.BlockSpec((step, width // pairs), lambda i, meta: (i, 0))] * pairs,
        ),
        compiler_params=pltpu.CompilerParams(vmem_limit_bytes=60 * MIB),
        cost_estimate=SMALL,
    )(meta, hidden, gain[None], bias[None])


def weave_kernel(meta_ref, q_ref, kv_ref, taken_q_ref, taken_kv_ref, *refs, cuts, behind):
    (out_ref,) = refs[behind:]

    def weave(queries_ref, keyval_ref):
        at = 0
        for first, last in cuts:
            for kind in range(3):
                cols = pl.ds(first * HEAD, (last - first) * HEAD)
                part = queries_ref[:, cols] if kind == 0 else keyval_ref[:, kind - 1, cols]
                out_ref[:, pl.ds(at, (last - first) * HEAD)] = part
                at += (last - first) * HEAD

    @pl.when(pl.program_id(0) == 0)
    def _():
        weave(q_ref, kv_ref)

    @pl.when(pl.program_id(0) != 0)
    def _():
        weave(taken_q_ref, taken_kv_ref)


def weave(core, w_query, w_keyval, taken_query, taken_keyval, cuts, behind):
    rows, cols = w_query.shape
    half = cols // 2
    step = 128 if rows % 128 == 0 else 64
    steps = rows // step
    own = lambda side, i, meta: jnp.where(side == 0, i, steps - 1)
    other = lambda side, i, meta: jnp.where(side == 0, 0, i)
    specs = []
    for place in (own, other):
        specs.append(pl.BlockSpec((step, half), lambda side, i, meta, place=place: (place(side, i, meta), meta[0])))
        specs.append(pl.BlockSpec((step, 2, half), lambda side, i, meta, place=place: (place(side, i, meta), 0, meta[0])))
    return pl.pallas_call(
        functools.partial(weave_kernel, cuts=cuts, behind=len(behind)),
        out_shape=jax.ShapeDtypeStruct((2 * rows, 3 * half), BF16),
        grid_spec=pltpu.PrefetchScalarGridSpec(
            num_scalar_prefetch=1,
            grid=(2, steps),
            in_specs=specs + [pl.BlockSpec(memory_space=pl.ANY)] * len(behind),
            out_specs=pl.BlockSpec((step, 3 * half), lambda side, i, meta: ((meta[0] ^ side) * steps + i, 0)),
        ),
        compiler_params=pltpu.CompilerParams(vmem_limit_bytes=60 * MIB),
        cost_estimate=SMALL,
    )(core.reshape(1).astype(jnp.int32), w_query, w_keyval, taken_query, taken_keyval, *behind)


def fetch_kernel(*refs, count, behind):
    out_refs, sem = refs[count + behind : -1], refs[-1]
    copies = [pltpu.make_async_copy(refs[at], out_refs[at], sem.at[at]) for at in range(count)]
    for copy in copies:
        copy.start()
    for copy in copies:
        copy.wait()


def fetch(sources, behind):
    space = pl.BlockSpec(memory_space=pl.ANY)
    return pl.pallas_call(
        functools.partial(fetch_kernel, count=len(sources), behind=len(behind)),
        out_shape=[jax.ShapeDtypeStruct(source.shape, source.dtype) for source in sources],
        in_specs=[space] * (len(sources) + len(behind)),
        out_specs=[pl.BlockSpec(memory_space=pltpu.VMEM)] * len(sources),
        scratch_shapes=[pltpu.SemaphoreType.DMA((len(sources),))],
        compiler_params=pltpu.CompilerParams(vmem_limit_bytes=60 * MIB),
        cost_estimate=SMALL,
    )(*sources, *behind)


def swap(value, axis, mask, size):
    return lax.ppermute(value, axis, [(i, i ^ mask) for i in range(size)])


def gather_block(table, places, dst, sem):
    for at, place in enumerate(places):

        @pl.when(table == at)
        def _(place=place):
            pltpu.make_async_copy(place, dst, sem).start()


def project_kernel(meta_ref, *refs, blocks, group, orders, behind):
    x_refs, w_ref = refs[:blocks], refs[blocks]
    out_refs, (x_buf, w_buf, x_sem, w_sem) = refs[blocks + 1 + behind : -4], refs[-4:]
    cols = w_buf.shape[1] // 3
    load = pltpu.make_async_copy(w_ref.at[:, pl.ds(group * 3 * cols, 3 * cols)], w_buf, w_sem)
    load.start()
    sequence = sorted(range(blocks), key=lambda e: -sum(bool(e >> order[0] & 1) for order in orders))
    for at, e in enumerate(sequence):
        gather_block(meta_ref[e], x_refs, x_buf.at[at], x_sem.at[at])
    load.wait()
    group_len = x_buf.shape[1]
    batch = 2
    for start in range(0, blocks, batch):
        for at in range(start, start + batch):
            pltpu.make_async_copy(x_refs[0], x_buf.at[at], x_sem.at[at]).wait()
        tokens = x_buf[start : start + batch].reshape(batch * group_len, x_buf.shape[2])
        product = jnp.dot(tokens, w_buf[...], preferred_element_type=F32).astype(BF16)
        first = 0
        for p, order in enumerate(orders):
            keep_ref, send_ref = out_refs[2 * p], out_refs[2 * p + 1]
            count = keep_ref.shape[2] // (3 * HEAD)
            ranked = slots_in(blocks, order)
            for c in range(batch):
                place = ranked.index(sequence[start + c])
                ref = keep_ref if place < blocks // 2 else send_ref
                for h in range(count):
                    for kind in range(3):
                        at = kind * cols + (first + h) * HEAD
                        ref[place % (blocks // 2), :, pl.ds((3 * h + kind) * HEAD, HEAD)] = product[
                            c * group_len : (c + 1) * group_len, at : at + HEAD
                        ]
            first += count


def slots_in(blocks, order):
    return sorted(range(blocks), key=lambda e: [e >> bit & 1 for bit in order] + [e & 1])


def project(meta, x_blocks, weights, group, per_group, orders, counts, behind):
    blocks = len(x_blocks)
    group_len, depth = x_blocks[0].shape
    any_space = pl.BlockSpec(memory_space=pl.ANY)
    out_shape = []
    for count in counts:
        out_shape += [jax.ShapeDtypeStruct((blocks // 2, group_len, count * 3 * HEAD), BF16)] * 2
    cols = per_group * 3 * HEAD
    return pl.pallas_call(
        functools.partial(project_kernel, blocks=blocks, group=group, orders=orders, behind=len(behind)),
        out_shape=out_shape,
        in_specs=[pl.BlockSpec(memory_space=pltpu.SMEM)] + [any_space] * (blocks + 1 + len(behind)),
        out_specs=[pl.BlockSpec(memory_space=pltpu.VMEM)] * len(out_shape),
        scratch_shapes=[
            pltpu.VMEM((blocks, group_len, depth), BF16),
            pltpu.VMEM((depth, cols), BF16),
            pltpu.SemaphoreType.DMA((blocks,)),
            pltpu.SemaphoreType.DMA(()),
        ],
        compiler_params=pltpu.CompilerParams(vmem_limit_bytes=48 * MIB),
        cost_estimate=SMALL,
    )(meta, *x_blocks, weights, *behind)


def forward_kernel(*refs, parts, terms, behind):
    out_refs = refs[parts * terms + behind :]
    for p in range(parts):
        mine = refs[p * terms : (p + 1) * terms]
        out_refs[p][...] = sum(ref[...].astype(F32) for ref in mine).astype(BF16)


def forward(terms, behind):
    left = min(t.shape[0] for t in terms[0]) // 2
    shapes = [(left, *ts[0].shape[1:]) for ts in terms]
    specs = [pl.BlockSpec(shape, lambda i: (1, 0, 0)) for shape, ts in zip(shapes, terms) for _ in ts]
    return pl.pallas_call(
        functools.partial(forward_kernel, parts=len(terms), terms=len(terms[0]), behind=len(behind)),
        grid=(1,),
        out_shape=[jax.ShapeDtypeStruct(shape, BF16) for shape in shapes],
        in_specs=specs + [pl.BlockSpec(memory_space=pl.ANY)] * len(behind),
        out_specs=[pl.BlockSpec(shape, lambda i: (0, 0, 0)) for shape in shapes],
        compiler_params=pltpu.CompilerParams(vmem_limit_bytes=60 * MIB),
        cost_estimate=SMALL,
    )(*[t for ts in terms for t in ts], *behind)


def settle_kernel(bias_ref, scale_ref, *refs, parts, terms, behind):
    mine_ref, theirs_ref = refs[parts * terms + behind :]
    width = mine_ref.shape[2]
    head = 0
    for p in range(parts):
        for h in range(refs[p * terms].shape[2] // width):
            cols = pl.ds(h * width, width)
            for e, ref in enumerate((mine_ref, theirs_ref)):
                total = sum(t[e, :, cols].astype(F32) for t in refs[p * terms : (p + 1) * terms])
                ref[head] = ((total + bias_ref[head : head + 1, :]) * scale_ref[...]).astype(BF16)
            head += 1


def settle(terms, bias, scale, behind):
    heads, width = bias.shape
    rows = terms[0][0].shape[1]
    specs = [pl.BlockSpec((2, *t.shape[1:]), lambda i: (0, 0, 0)) for ts in terms for t in ts]
    whole = pl.BlockSpec((heads, rows, width), lambda i: (0, 0, 0))
    return pl.pallas_call(
        functools.partial(settle_kernel, parts=len(terms), terms=len(terms[0]), behind=len(behind)),
        grid=(1,),
        out_shape=[jax.ShapeDtypeStruct((heads, rows, width), BF16)] * 2,
        in_specs=[pl.BlockSpec((heads, width), lambda i: (0, 0)), pl.BlockSpec((1, width), lambda i: (0, 0))]
        + specs
        + [pl.BlockSpec(memory_space=pl.ANY)] * len(behind),
        out_specs=[whole, whole],
        compiler_params=pltpu.CompilerParams(vmem_limit_bytes=60 * MIB),
        cost_estimate=SMALL,
    )(bias, scale, *[t for ts in terms for t in ts], *behind)


def attend_kernel(meta_ref, own_ref, other_ref, k_ref, v_ref, *refs, key_len, behind):
    o_ref, nk_ref, nv_ref = refs[behind:]
    length = meta_ref[0]
    qkv = jnp.where(pl.program_id(0) < pl.num_programs(0) // 2, own_ref[0], other_ref[0])
    q, new_k, new_v = qkv[:, :HEAD], qkv[:, HEAD : 2 * HEAD], qkv[:, 2 * HEAD :]
    nk_ref[...] = new_k
    nv_ref[...] = new_v
    group = q.shape[0]
    cache_len = k_ref.shape[1]

    def scores_of(at):
        keys = k_ref[0, at : at + key_len, :]
        scores = lax.dot_general(q, keys, (((1,), (1,)), ((), ())), preferred_element_type=F32)
        positions = at + lax.broadcasted_iota(jnp.int32, (1, key_len), 1)
        return jnp.where(positions < length, scores, -1e30)

    def lane_sum(probs):
        total = probs[:, :HEAD]
        for at in range(HEAD, probs.shape[1], HEAD):
            total = total + probs[:, at : at + HEAD]
        return total

    rows = lax.broadcasted_iota(jnp.int32, (group, group), 0)
    cols = lax.broadcasted_iota(jnp.int32, (group, group), 1)
    scores = lax.dot_general(q, new_k, (((1,), (1,)), ((), ())), preferred_element_type=F32)
    scores = jnp.where(cols <= rows, scores, -1e30)
    following = scores_of(0)
    row_max = jnp.max(scores, axis=1, keepdims=True)
    probs = jnp.exp(scores - row_max)
    row_sum = lane_sum(probs)
    weighted = jnp.dot(probs.astype(BF16), new_v, preferred_element_type=F32)
    for at in range(0, cache_len, key_len):
        scores = following
        if at + key_len < cache_len:
            following = scores_of(at + key_len)
        new_max = jnp.maximum(row_max, jnp.max(scores, axis=1, keepdims=True))
        factor = jnp.exp(row_max - new_max)
        probs = jnp.exp(scores - new_max)
        row_max = new_max
        row_sum = row_sum * factor + lane_sum(probs)
        values = v_ref[0, at : at + key_len, :]
        weighted = weighted * factor + jnp.dot(probs.astype(BF16), values, preferred_element_type=F32)
    total = jnp.sum(row_sum, axis=1, keepdims=True)
    o_ref[...] = (weighted / total).astype(BF16)


def attend(meta, own, other, cache_k, cache_v, base, half, behind):
    count, group, width = own.shape
    heads = 2 * count
    cache_len = cache_k.shape[1]
    key_len = min(512, cache_len)

    def side(i, meta):
        return (i // count) ^ meta[1]

    cached = pl.BlockSpec((1, cache_len, HEAD), lambda i, meta: (0, 0, side(i, meta) * half + base + i % count))
    placed = pl.BlockSpec((group, HEAD), lambda i, meta: (0, side(i, meta) * count + i % count))
    return pl.pallas_call(
        functools.partial(attend_kernel, key_len=key_len, behind=len(behind)),
        out_shape=[jax.ShapeDtypeStruct((group, heads * HEAD), BF16)] * 3,
        grid_spec=pltpu.PrefetchScalarGridSpec(
            num_scalar_prefetch=1,
            grid=(heads,),
            in_specs=[
                pl.BlockSpec((1, group, width), lambda i, meta: (jnp.minimum(i, count - 1), 0, 0)),
                pl.BlockSpec((1, group, width), lambda i, meta: (jnp.maximum(i - count, 0), 0, 0)),
                cached,
                cached,
            ]
            + [pl.BlockSpec(memory_space=pl.ANY)] * len(behind),
            out_specs=[placed] * 3,
        ),
        compiler_params=pltpu.CompilerParams(vmem_limit_bytes=48 * MIB),
        cost_estimate=SMALL,
    )(meta, own, other, cache_k, cache_v, *behind)


def output_kernel(*refs, pairs, groups):
    a_refs = [refs[g * pairs : (g + 1) * pairs] for g in range(groups)]
    w_refs = refs[groups * pairs : groups * pairs + 2]
    out_refs, (buf, sem) = refs[groups * pairs + 2 : -2], refs[-2:]
    _, rows, head_cols = buf.shape
    half = head_cols // 2
    cols = half // groups
    chunk = rows // len(out_refs)
    for d in range(pairs):
        for g in range(groups):
            for side in range(2):
                pltpu.make_async_copy(
                    a_refs[g][d].at[:, pl.ds(side * cols, cols)],
                    buf.at[d, :, pl.ds(side * half + g * cols, cols)],
                    sem.at[d],
                ).start()
    for d in range(pairs):
        pltpu.make_async_copy(buf.at[d], buf.at[d], sem.at[d]).wait()
    for d in range(0, pairs, 2):
        tokens = buf[d : d + 2].reshape(2 * rows, head_cols)
        for j in range(2):
            product = jnp.dot(tokens, w_refs[j][...], preferred_element_type=F32).astype(BF16)
            for c, out_ref in enumerate(out_refs):
                for at in range(2):
                    first = at * rows + c * chunk
                    out_ref[j, d + at] = product[first : first + chunk]


def output(gathered, w_pair, chunks):
    groups, pairs = len(gathered), len(gathered[0])
    rows = gathered[0][0].shape[0]
    head_cols, out_cols = w_pair[0].shape
    space = pl.BlockSpec(memory_space=pl.ANY)
    vmem = pl.BlockSpec(memory_space=pltpu.VMEM)
    return pl.pallas_call(
        functools.partial(output_kernel, pairs=pairs, groups=groups),
        out_shape=[jax.ShapeDtypeStruct((2, pairs, rows // chunks, out_cols), BF16)] * chunks,
        in_specs=[space] * (groups * pairs) + [vmem] * 2,
        out_specs=[vmem] * chunks,
        scratch_shapes=[pltpu.VMEM((pairs, rows, head_cols), BF16), pltpu.SemaphoreType.DMA((pairs,))],
        compiler_params=pltpu.CompilerParams(vmem_limit_bytes=40 * MIB),
        cost_estimate=SMALL,
    )(*[a for part in gathered for a in part], *w_pair)


def block_call(kernel, out_shapes, scalars, arrays, shapes, indices, behind):
    return pl.pallas_call(
        functools.partial(kernel, behind=len(behind)),
        out_shape=[jax.ShapeDtypeStruct(shape, BF16) for shape in out_shapes],
        grid_spec=pltpu.PrefetchScalarGridSpec(
            num_scalar_prefetch=1,
            grid=(1,),
            in_specs=[pl.BlockSpec(shape, index) for shape, index in zip(shapes, indices)]
            + [pl.BlockSpec(memory_space=pl.ANY)] * len(behind),
            out_specs=[
                pl.BlockSpec(shape, lambda i, meta, rank=len(shape): (0,) * rank) for shape in out_shapes
            ],
        ),
        compiler_params=pltpu.CompilerParams(vmem_limit_bytes=16 * MIB),
        cost_estimate=SMALL,
    )(scalars, *arrays, *behind)


def split_pair_kernel(meta_ref, own_ref, came_ref, *refs, behind):
    mine_ref, sent_ref = refs[behind:]
    count = mine_ref.shape[1]
    pairs = 2 * count
    offsets = slots_in(2 * pairs, range(1, pairs.bit_length()))[::2]
    for at, e in enumerate(offsets):
        place = meta_ref[e]
        for j in range(2):
            block = jnp.where(place % 2 == 0, own_ref[j, place // 2], came_ref[1 - j, place // 2])
            if at < count:
                mine_ref[j, at] = block
            else:
                sent_ref[j, at - count] = block


def split_pair(places, own, came, behind):
    _, pairs, chunk, cols = own.shape
    first = lambda i, meta: (0, 0, 0, 0)
    shapes = [(2, pairs // 2, chunk, cols)] * 2
    return block_call(split_pair_kernel, shapes, places, [own, came], [own.shape] * 2, [first] * 2, behind)


def choose_kernel(meta_ref, keep_ref, came_ref, *refs, behind):
    mine_ref, sent_ref = refs[behind:]

    @pl.when(meta_ref[0] == 0)
    def _():
        mine_ref[...] = keep_ref[...]
        sent_ref[...] = came_ref[...]

    @pl.when(meta_ref[0] != 0)
    def _():
        mine_ref[...] = came_ref[...]
        sent_ref[...] = keep_ref[...]


def choose(flip, keep, came, behind):
    first = lambda i, meta: (0,) * keep.ndim
    return block_call(choose_kernel, [keep.shape] * 2, flip, [keep, came], [keep.shape] * 2, [first] * 2, behind)


def add_split_kernel(meta_ref, keep_ref, came_ref, *refs, behind):
    mine_ref, sent_ref = refs[behind:]
    count = mine_ref.shape[1]
    total = (keep_ref[...].astype(F32) + came_ref[...].astype(F32)).astype(BF16)
    mine_ref[...] = total[:, :count]
    sent_ref[...] = total[:, count:]


def add_split(keep, came, behind):
    slices, count, chunk, cols = keep.shape
    first = lambda i, meta: (0, 0, 0, 0)
    shapes = [(slices, count // 2, chunk, cols)] * 2
    scalars = jnp.zeros((1,), jnp.int32)
    return block_call(add_split_kernel, shapes, scalars, [keep, came], [keep.shape] * 2, [first] * 2, behind)


def finish_rows_kernel(meta_ref, keep_ref, came_ref, hidden_ref, bias_ref, *refs, behind):
    (out_ref,) = refs[behind:]
    cols = keep_ref.shape[3]
    total = [keep_ref[j, 0].astype(F32) + came_ref[j, 0].astype(F32) for j in range(2)]
    for side in range(2):
        at = pl.ds(side * cols, cols)
        part = jnp.where(meta_ref[0] == side, total[0], total[1])
        out_ref[:, at] = (part + bias_ref[:, at] + hidden_ref[:, at].astype(F32)).astype(BF16)


def finish_rows(meta, keep, came, hidden, bias, at, behind):
    chunk, cols = keep.shape[2:]
    width = 2 * cols
    shapes = [keep.shape, keep.shape, (chunk, width), (1, width)]
    first = lambda i, meta: (0, 0, 0, 0)
    indices = [first, first, lambda i, meta: (at, meta[1]), lambda i, meta: (0, 0)]
    arrays = [keep, came, hidden, bias[None]]
    return block_call(finish_rows_kernel, [(chunk, width)], meta, arrays, shapes, indices, behind)[0]


def local(
    rows_n,
    cols_n,
    hidden_in,
    norm_gain,
    norm_bias,
    w_query,
    w_keyval,
    bias_query,
    bias_keyval,
    cache_keys,
    cache_values,
    cache_lengths,
    owner_slot,
    w_out,
    bias_out,
):
    row = lax.axis_index("row")
    col = lax.axis_index("col")
    core = row & 1
    group_len, width = hidden_in.shape
    slice_len, head_cols = w_query.shape
    half = head_cols // HEAD // 2
    half_cols = head_cols // 2
    pairs = rows_n // 2
    row_bits = rows_n.bit_length() - 1
    col_bits = cols_n.bit_length() - 1
    q_scale = HEAD ** (-0.5)
    slot_ids = jnp.arange(rows_n, dtype=jnp.int32)
    is_owner = owner_slot[:, None] == slot_ids[None, :]
    inverse = jnp.sum(jnp.where(is_owner, slot_ids[:, None], 0), axis=0).astype(jnp.int32)

    pair = row // 2
    pieces = normalize(pair.reshape(1).astype(jnp.int32), hidden_in, norm_gain, norm_bias, pairs)
    x_blocks = [None] * rows_n
    for offset in reversed(range(pairs)):
        piece = swap(pieces[offset], "row", 2 * offset, rows_n) if offset else pieces[0]
        x_blocks[2 * offset] = piece

    groups = 3 if half % 3 == 0 else 1
    per_group = half // groups
    parts = [(g * per_group, (g + 1) * per_group) for g in range(groups)]
    taken = swap(w_query, "row", 1, rows_n), swap(w_keyval, "row", 1, rows_n)
    weights = weave(core, w_query, w_keyval, *taken, parts, [pieces[0]])
    arrived = fetch(x_blocks[::2], [weights])
    for offset in range(pairs):
        x_blocks[2 * offset + 1] = swap(arrived[offset], "row", 1, rows_n)

    bias = jnp.concatenate([bias_query[None], bias_keyval], axis=0).reshape(3, 2, half, HEAD).transpose(1, 2, 0, 3)
    bias = lax.dynamic_index_in_dim(bias, core, 0, keepdims=False).reshape(half, 3 * HEAD)
    scale = jnp.concatenate([jnp.full((HEAD,), q_scale, F32), jnp.ones((2 * HEAD,), F32)])

    counts = [per_group // 2, per_group - per_group // 2] if per_group > 1 else [1]
    pair_bits = list(range(1, row_bits))
    orders = [pair_bits[at % len(pair_bits) :] + pair_bits[: at % len(pair_bits)] for at in range(len(counts))]
    project_meta = (inverse[row ^ slot_ids] ^ row).astype(jnp.int32)
    attend_meta = jnp.stack([cache_lengths[inverse[row]], core]).astype(jnp.int32)

    def project_group(g, behind):
        return project(project_meta, x_blocks, weights, g, per_group, orders, counts, behind)

    projected = [project_group(0, [])]
    w_pair = w_out, swap(fetch([w_out], projected[0][:1])[0], "row", 1, rows_n)
    key_parts, value_parts, gathered, finished, waiting = [], [], [], [], []

    def finish(g):
        base = g * per_group
        mine, theirs = settle(
            waiting[g],
            bias[base : base + per_group],
            scale[None],
            finished[-1:] + ([projected[g + 2][0]] if g + 2 < groups else [])
            + ([sent] if g + 1 < groups else []),
        )
        came = swap(theirs, "row", 1, rows_n)
        attended, new_k, new_v = attend(
            attend_meta, mine, came, cache_keys, cache_values, base, half, []
        )
        finished.append(attended)
        key_parts.append(new_k)
        value_parts.append(new_v)
        gathered.append([swap(attended, "row", 2 * d, rows_n) if d else attended for d in range(pairs)])

    for g in range(groups):
        terms = [[projected[g][2 * p]] for p in range(len(orders))]
        sends = [projected[g][2 * p + 1] for p in range(len(orders))]
        if g + 1 < groups:
            projected.append(project_group(g + 1, [sent] if g else [projected[0][0], w_pair[1]]))
        for at in range(len(pair_bits)):
            for p, order in enumerate(orders):
                terms[p].append(swap(sends[p], "row", 1 << order[at], rows_n))
            if at + 1 < len(pair_bits):
                sends = forward(terms, finished[-1:] + ([projected[g + 1][0]] if g + 1 < groups else []))
                sent = sends[0]
        waiting.append(terms)
        if g:
            finish(g - 1)
    finish(groups - 1)

    cols = per_group * HEAD
    new_k, new_v = (
        jnp.concatenate([p[:, side * cols : (side + 1) * cols] for side in range(2) for p in parts], axis=1)[None]
        for parts in (key_parts, value_parts)
    )

    places = (owner_slot[row ^ slot_ids] ^ row).astype(jnp.int32)
    shift = row_bits - col_bits
    if shift != 1:
        raise ValueError("unexpected mesh")
    chunks = 4
    chunk = group_len // chunks
    last = row_bits - 1
    flips = [((row >> bit) ^ (col >> (bit - 1))) & 1 for bit in range(1, row_bits)]
    flips = [flip.reshape(1).astype(jnp.int32) for flip in flips]
    final_meta = jnp.stack([core, col]).astype(jnp.int32)
    late = [0, 0] + [at for bit in range(1, last) for at in (4.5 * bit + 1.5, 4.5 * bit + 4.5)]
    late += [4.5 * last + 1.5, 4.5 * last + 2.8]
    order = sorted((c * (2 if step > 1 else 0.5) + late[step], step, c) for c in range(chunks) for step in range(1, 2 * last + 2))
    products = output(gathered, w_pair, chunks)
    state = {c: (product, swap(product, "row", 1, rows_n)) for c, product in enumerate(products)}
    done, order_behind = {}, []
    for _, step, c in order:
        if step == 2 * last + 1:
            done[c] = finish_rows(final_meta, *state[c], hidden_in, bias_out, c, order_behind)
            order_behind = [done[c]]
        else:
            bit = (step + 1) // 2
            if step == 1:
                keep, sent = split_pair(places, *state[c], order_behind)
            elif step % 2:
                keep, sent = add_split(*state[c], order_behind)
            else:
                keep, sent = choose(flips[bit - 1], *state[c], order_behind)
            axis, mask, size = ("row", 1 << bit, rows_n) if step % 2 else ("col", 1 << (bit - 1), cols_n)
            state[c] = (keep, swap(sent, axis, mask, size))
            order_behind = [sent]
    hidden_out = jnp.concatenate([done[c] for c in range(chunks)], axis=0)
    return hidden_out, new_k, new_v


def solution(mesh):
    placed = (
        P("row", None),
        P(),
        P(),
        P("row", "col"),
        P("row", None, "col"),
        P("col"),
        P(None, "col"),
        P("row", None, "col"),
        P("row", None, "col"),
        P(),
        P(),
        P("col", "row"),
        P("col"),
    )
    return jax.shard_map(
        functools.partial(local, mesh.shape["row"], mesh.shape["col"]),
        mesh=mesh,
        in_specs=placed,
        out_specs=(P("row", "col"), P("row", None, "col"), P("row", None, "col")),
        check_vma=False,
    )
```
